128 devices in a mesh: row: 8 (over x, core), col: 16 (over y, z).
Axes of the slice: x: 4, y: 4, z: 4, core: 2. Of those that a mesh axis runs over, the one named last changes fastest.
Arguments:
- iterate: bfloat16 [5120, 20480], P('col', 'row'), may hold values from -3.59375 to 3.59375
- route: int32 [5120, 1], P('col'), may hold values from 0 to 7; in each aligned block of 320 rows (0 to 319, 320 to 639, ...) at most 42 rows name the same one
Outputs:
- update: bfloat16 [5376, 20480], P('row', 'col')
The draws below stay inside these ranges and needn't reach their ends.
Inputs may be any that keep to these rules, and one draw needn't show every extreme that they name: `route`: in the rows of one FSDP shard (aligned blocks of 320 rows) no grid row block is named by more than 42 rows, and some shard names one exactly 42 times.
All inputs are finite; a program needn't handle non-finite values.
Results may differ from the reference program's by a relative error of at most 0.017.
Values may be sent and summed in bfloat16 or wider, within the bound.
No kernel may reach another device: no remote copies, remote signals or barrier semaphores. Data moves between devices by JAX's collectives and lax.ppermute only.
A program may use at most 128 MiB of HBM per device.

```python
import math
import jax
import jax.numpy as jnp
import numpy as np
from jax import lax

ROWS = 5120
COLS = 20480
SHARD = 320
MOST = 42
GROUP = 672
SLOTS = 5376
N_ROW = 8
N_COL = 16


def block_scale(rng, extent, pieces, smallest, high):
    def one(axis_at, parts):
        draws = jax.random.uniform(jax.random.fold_in(jax.random.fold_in(rng, 6), axis_at), (parts,), jnp.float32, smallest / len(pieces), high / len(pieces))
        return jnp.repeat(jnp.exp(draws), extent[axis_at] // parts).reshape((-1,) + (1,) * (len(extent) - axis_at - 1))

    loudness = one(*pieces[0])
    for cut in pieces[1:]:
        loudness = loudness * one(*cut)
    return loudness


def deal_out(stream_key, own, number, rows, number_of, top, limit, skew):
    sequence = jax.random.permutation(stream_key, number_of)
    packed, common = portions_of(number_of, rows * top, limit, skew, True), portions_of(number_of, rows * top, limit, skew, False)
    places = jnp.arange(number_of)

    def named(lengths, rotation):
        used = int((lengths > 0).sum())
        fixed = max(1, used // 4)
        passed = fixed + (places - fixed + rotation * (used - fixed)) % max(1, number_of - fixed)
        return jnp.zeros((number_of,), jnp.int32).at[sequence[jnp.where(places < fixed, places, passed)]].set(jnp.asarray(lengths, jnp.int32))

    lengths = jnp.where(number % 4 == 0, named(packed, number // 4), named(common, number - number // 4 - 1))
    mixed = jax.random.permutation(jax.random.fold_in(own, 3), number_of)
    donor, sink = mixed[0:number_of // 2 * 2:2], mixed[1:number_of // 2 * 2:2]
    slack = jnp.minimum(lengths[donor] - 1, limit - lengths[sink]) // 2
    slack = jnp.where((donor == sequence[0]) | (sink == sequence[0]) | (lengths[sink] == 0), 0, jnp.maximum(slack, 0))
    passed = jax.random.randint(jax.random.fold_in(own, 4), (number_of // 2,), 0, 1 << 20) % (slack + 1)
    lengths = lengths.at[donor].add(-passed).at[sink].add(passed)
    members = jnp.searchsorted(jnp.cumsum(lengths), jnp.arange(rows * top), side="right").astype(jnp.int32)
    listing = members.reshape(top, rows).T
    listing = listing[jax.random.permutation(jax.random.fold_in(own, 1), rows)]
    rotation = jax.random.randint(jax.random.fold_in(own, 2), (rows, 1), 0, top)
    return jnp.take_along_axis(listing, (jnp.arange(top)[None, :] + rotation) % top, axis=1)


def portions_of(number_of, total, limit, lean, full):
    loads = [(1 << 20) // math.isqrt(rank ** lean) + 1 for rank in range(1, number_of + 1)]
    largest = limit if full else min(limit, max(-(-total // number_of), total * loads[0] // sum(loads)))
    least = 1 if total - largest >= number_of - 1 else 0
    given, spare = [largest] + [least] * (number_of - 1), total - largest - least * (number_of - 1)
    while spare > 0:
        free = [i for i in range(1, number_of) if given[i] < largest] or [i for i in range(1, number_of) if given[i] < limit]
        mass, remaining = sum([loads[i] for i in free]), spare
        for i in free:
            more = min(limit - given[i], max(1, remaining * loads[i] // mass), spare)
            given[i] = given[i] + more
            spare = spare - more
    return np.array(given)


def gaussian(key, shape, spread, most, pieces=(), kind=jnp.bfloat16):
    drawn = jax.random.normal(key, shape, jnp.float32) * spread
    if len(pieces) > 0:
        drawn = block_scale(key, shape, pieces, -0.22, 0.18) * drawn
    return jnp.clip(drawn, min=-most, max=most).astype(kind)


def setup_inputs(seed: int = 0) -> dict:
    key_list = jax.random.split(jax.random.key(seed), 3)
    iterate = gaussian(key_list[0], (ROWS, COLS), 0.6, 3.59375, ((0, 16), (1, 8)))
    route_keys = jax.random.split(jax.random.fold_in(key_list[1], 1), ROWS // SHARD)
    route_turns = jax.random.permutation(jax.random.fold_in(key_list[1], 3), ROWS // SHARD)
    route = jax.vmap(lambda own, number: deal_out(jax.random.fold_in(key_list[1], 2), own, number, SHARD, N_ROW, 1, MOST, 0))(route_keys, route_turns).reshape((ROWS, 1))
    return dict(iterate=iterate, route=route)


coef_first = 3.4445
coef_second = -4.7750
coef_third = 2.0315


def place(iterate, route):
    target = route[:, 0].astype(jnp.int32).reshape(N_COL, SHARD)
    labels = jnp.arange(N_ROW, dtype=jnp.int32)
    onehot = (target[:, :, None] == labels[None, None, :]).astype(jnp.int32)
    before = jnp.cumsum(onehot, axis=1) - onehot
    position = jnp.sum(before * onehot, axis=2).astype(jnp.int32)
    source = jnp.arange(N_COL, dtype=jnp.int32)[:, None]
    slot_index = (target * GROUP + source * MOST + position).reshape(-1).astype(jnp.int32)
    return jnp.zeros((SLOTS, COLS), jnp.bfloat16).at[slot_index].set(iterate)


def reference(iterate, route):
    placed = place(iterate, route)
    width = COLS // N_COL

    def add_block(step, total):
        start = (step * width).astype(jnp.int32)
        piece = lax.dynamic_slice_in_dim(placed, start, width, 1)
        term = lax.dot_general(piece, piece, (((1,), (1,)), ((), ())), preferred_element_type=jnp.float32) * (1.0 / COLS)
        rounded = lax.optimization_barrier(term.astype(jnp.bfloat16))
        return total + rounded.astype(jnp.float32)

    total = lax.fori_loop(0, N_COL, add_block, jnp.zeros((SLOTS, SLOTS), jnp.float32))
    gram = total.astype(jnp.bfloat16)
    square = jnp.dot(gram, gram, preferred_element_type=jnp.float32).astype(jnp.bfloat16)
    mixer = (coef_second * gram.astype(jnp.float32) + coef_third * square.astype(jnp.float32)).astype(jnp.bfloat16)
    product = jnp.dot(mixer, placed, preferred_element_type=jnp.float32)
    return (coef_first * placed.astype(jnp.float32) + product).astype(jnp.bfloat16)
```

```python
import jax
import jax.numpy as jnp
from jax import lax
from jax.experimental import pallas as pl
from jax.experimental.pallas import tpu as pltpu
from jax.sharding import PartitionSpec as P

coef_first = 3.4445
coef_second = -4.775
coef_third = 2.0315

N_X, N_CORE, N_Y, N_Z = 4, 2, 4, 4
PAD = 48
BF = jnp.bfloat16
F32 = jnp.float32


def row_perm(dx, flip):
    return [
        (x * 2 + k, ((x + dx) % 4) * 2 + (k ^ flip)) for x in range(4) for k in range(2)
    ]


def col_perm(dy, dz):
    return [
        (y * 4 + z, ((y + dy) % 4) * 4 + (z + dz) % 4) for y in range(4) for z in range(4)
    ]


def send_x(a, d):
    return lax.ppermute(a, "row", row_perm(d, 0))


def swap_core(a):
    return lax.ppermute(a, "row", row_perm(0, 1))


def send_y(a, d):
    return lax.ppermute(a, "col", col_perm(d, 0))


def send_z(a, d):
    return lax.ppermute(a, "col", col_perm(0, d))


def ring_gather(a, send):
    half = a.shape[0] // 2
    plus = send(a, 1)
    minus = send(a, -1)
    first = send(plus[:half], 1)
    second = send(minus[half:], -1)
    return [a, plus, jnp.concatenate([first, second], axis=0), minus]


def pick(a, index, axis):
    return lax.dynamic_index_in_dim(a, index % 4, axis=axis, keepdims=False)


def ring_scatter(a, send, index, axis):
    own = pick(a, index, axis)
    plus = send(pick(a, index + 1, axis), 1)
    minus = send(pick(a, index - 1, axis), -1)
    far = send(pick(a, index + 2, axis), 2)
    total = own.astype(F32) + plus.astype(F32) + minus.astype(F32) + far.astype(F32)
    return total.astype(BF)


def sync(*arrays):
    return lax.optimization_barrier(arrays)


def plane_gather(a, b):
    a_z, b_y = sync_ring(a, send_z, b, send_y)
    a_z, b_y = jnp.concatenate(a_z, axis=0), jnp.concatenate(b_y, axis=0)
    return sync_ring(a_z, send_y, b_y, send_z)


def sync_ring(a, send_a, b, send_b):
    half_a, half_b = a.shape[0] // 2, b.shape[0] // 2
    plus_a, minus_a, plus_b, minus_b = sync(
        send_a(a, 1), send_a(a, -1), send_b(b, 1), send_b(b, -1)
    )
    far_a = [send_a(plus_a[:half_a], 1), send_a(minus_a[half_a:], -1)]
    far_b = [send_b(plus_b[:half_b], 1), send_b(minus_b[half_b:], -1)]
    return (
        [a, plus_a, jnp.concatenate(far_a, axis=0), minus_a],
        [b, plus_b, jnp.concatenate(far_b, axis=0), minus_b],
    )


def regroup_kernel(cols_ref, order_ref, *refs):
    blocks, (low, high) = refs[:8], refs[8:]
    for i in range(8):
        place = order_ref[i]

        @pl.when(place < 4)
        def _():
            low[0, place] = blocks[i][0]

        @pl.when(place >= 4)
        def _():
            high[0, place - 4] = blocks[i][0]


def regroup(blocks, cols, order):
    count, rows, width = blocks[0].shape
    spec = pl.BlockSpec((1, rows, width), lambda j, c, o: (c[j], 0, 0))
    low_spec = pl.BlockSpec((1, 4, rows, width), lambda j, c, o: (j, 0, 0, 0))
    high_spec = pl.BlockSpec((1, 4, rows, width), lambda j, c, o: (j % 4 * 4 + j // 4, 0, 0, 0))
    shape = jax.ShapeDtypeStruct((count, 4, rows, width), blocks[0].dtype)
    return pl.pallas_call(
        regroup_kernel,
        grid_spec=pltpu.PrefetchScalarGridSpec(
            num_scalar_prefetch=2,
            grid=(count,),
            in_specs=[spec] * 8,
            out_specs=[low_spec, high_spec],
        ),
        out_shape=[shape, shape],
        compiler_params=pltpu.CompilerParams(vmem_limit_bytes=32 * 1024 * 1024),
        cost_estimate=pl.CostEstimate(
            flops=0, bytes_accessed=4 * 8 * count * rows * width, transcendentals=0
        ),
    )(cols, order, *blocks)


def positions(match):
    return jnp.cumsum(match, axis=-1) - 1


def selector(target, group):
    match = (target == group).astype(jnp.int32)
    slot = lax.broadcasted_iota(jnp.int32, (PAD, 1), 0)
    return ((positions(match)[None, :] == slot) & (match[None, :] == 1)).astype(BF)


def body(iterate, route):
    rows, wide = iterate.shape
    groups, count = 8, 16
    q = rows // groups
    width = wide // 2
    scale = 1.0 / (wide * groups)
    capacity = 42
    ri, ci = lax.axis_index("row"), lax.axis_index("col")
    x, core, y, z = ri // 2, ri % 2, ci // 4, ci % 4

    parts = iterate.reshape(groups, q, 2, width).transpose(0, 2, 1, 3)
    parts = lax.all_to_all(parts, "row", 0, 0, tiled=True).reshape(count, q, width)
    own = lax.all_to_all(parts, "col", 0, 0, tiled=True).reshape(count * q, width)
    same = ring_gather(own, send_x)
    panels = [[s, swap_core(s)] for s in same]

    stage = [[], []]
    for d in (0, 1, 3, 2):
        for b in range(2):
            part = lax.dot_general(
                panels[d][b], own, (((1,), (1,)), ((), ())), preferred_element_type=F32
            )
            part = (part * scale).astype(BF).reshape(4, 4, q, groups * count * q // groups)
            if b == 0:
                stage[0].append((d, ring_scatter(part, send_y, y, 0)))
            else:
                stage[1].append((d, ring_scatter(part, send_z, z, 1)))
    shares = []
    for b, (send, index) in enumerate(((send_z, z), (send_y, y))):
        by_d = dict(stage[b])
        stacked = jnp.stack([by_d[d] for d in range(4)], axis=0)
        shares.append(ring_scatter(stacked, send, index, 1))
    flip = core == 1
    even = jnp.where(flip, shares[1], shares[0])
    odd = jnp.where(flip, shares[0], shares[1])
    ordered = jnp.stack(
        [v for t in range(4) for v in (pick(even, x - t, 0), pick(odd, x - t, 0))], axis=0
    )
    gram_share = ordered.reshape(rows, -1)

    choose = jnp.concatenate([selector(route[:, 0], g) for g in range(groups)], axis=0)
    routed = jnp.dot(choose, gram_share, preferred_element_type=F32).astype(BF)
    routed = routed.reshape(4, 2, PAD, -1)
    mine = jnp.where(flip, routed[:, 1], routed[:, 0])
    other = swap_core(jnp.where(flip, routed[:, 0], routed[:, 1]))
    routed = jnp.stack([mine, other], axis=1)
    arrived = sync(
        pick(routed, x, 0),
        send_x(pick(routed, x + 1, 0), 1),
        send_x(pick(routed, x + 2, 0), 2),
        send_x(pick(routed, x - 1, 0), -1),
    )
    lanes = [arrived[d][b] for d in range(4) for b in range(2)]
    chunks_a, chunks_b = plane_gather(
        jnp.concatenate(lanes[:4], axis=1), jnp.concatenate(lanes[4:], axis=1)
    )

    gram_same = ring_gather(gram_share, send_x)
    gram_blocks = [v for s in gram_same for v in (s, swap_core(s))]
    gram_a = jnp.concatenate(gram_blocks[:4], axis=1)
    gram_b = jnp.concatenate(gram_blocks[4:], axis=1)

    steps = jnp.arange(4, dtype=jnp.int32)
    order = jnp.stack([((x - d) % 4) * 2 + (core ^ b) for d in range(4) for b in range(2)])
    by_z = route.reshape(1, rows)
    by_z = jnp.stack([by_z, send_z(by_z, 1), send_z(by_z, 2), send_z(by_z, -1)], axis=1)
    targets = jnp.stack([by_z, send_y(by_z, 1), send_y(by_z, 2), send_y(by_z, -1)], axis=0)
    targets = targets.reshape(count, rows)
    shares_y, shares_z = (y - steps) % 4, (z - steps) % 4
    sources = (shares_y[:, None] * 4 + shares_z[None, :]).reshape(count)
    match = (targets == ri).astype(jnp.int32)
    slot_of = jnp.where(match == 1, sources[:, None] * capacity + positions(match), -1)
    slot_of = jnp.take(jnp.zeros_like(slot_of).at[sources].set(slot_of), jnp.arange(count), axis=0)
    slot_of = slot_of.reshape(count, groups, q).transpose(1, 0, 2)
    slot_of = jnp.take(slot_of, order, axis=0).reshape(1, groups * count * q)
    slots = capacity * count
    slot = lax.broadcasted_iota(jnp.int32, (slots, 1), 0)
    place = (slot == slot_of).astype(BF)

    half_k = 4 * count * q
    rows_rows = (((1,), (1,)), ((), ()))
    gram_cols = lax.dot_general(gram_a, place[:, :half_k], rows_rows, preferred_element_type=F32)
    gram_cols = gram_cols + lax.dot_general(
        gram_b, place[:, half_k:], rows_rows, preferred_element_type=F32
    )
    source, position = slot // capacity, slot % capacity
    away_y, away_z = (y - source // 4) % 4, (z - source % 4) % 4
    padded = lax.broadcasted_iota(jnp.int32, (1, count * PAD), 1)
    square = 0.0
    for chunks, gram, column in (
        (chunks_a, gram_a, (away_y * 4 + away_z) * PAD + position),
        (chunks_b, gram_b, (away_z * 4 + away_y) * PAD + position),
    ):
        terms = [
            lax.dot_general(v, gram, rows_rows, preferred_element_type=F32).astype(BF)
            for v in chunks
        ]
        compact = (padded == column).astype(BF)
        square = square + lax.dot_general(
            jnp.concatenate(terms, axis=0), compact, (((0,), (1,)), ((), ())), preferred_element_type=F32
        )
    square = square.astype(BF).astype(F32)
    mixer = (coef_second * gram_cols.astype(BF).astype(F32) + coef_third * square).astype(BF)
    half = rows // 2
    mixer_a, mixer_b = plane_gather(mixer[:half], mixer[half:])

    flat = [v for s in panels for v in s]
    low, high = regroup([v.reshape(count, q, width) for v in flat], sources, order)
    low = low.reshape(4, 4 * half, width)
    high = high.reshape(4, 4 * half, width)
    update = 0.0
    for i, v in enumerate(flat):
        update = update + jnp.dot(
            place[:, i * count * q : (i + 1) * count * q], v, preferred_element_type=F32
        )
    update = coef_first * update
    for j in (0, 1, 3, 2):
        for chunks, panel in ((mixer_a, low), (mixer_b, high)):
            update = update + lax.dot_general(
                chunks[j], panel[j], (((0,), (0,)), ((), ())), preferred_element_type=F32
            )
    return update.astype(BF)


def solution(mesh):
    in_specs = (P("col", "row"), P("col", None))
    out_specs = P("row", "col")
    return jax.shard_map(body, mesh=mesh, in_specs=in_specs, out_specs=out_specs, check_vma=False)
```

```python
import jax
import jax.numpy as jnp
from jax import lax
from jax.experimental import pallas as pl
from jax.experimental.pallas import tpu as pltpu
from jax.sharding import PartitionSpec as P

coef_first = 3.4445
coef_second = -4.775
coef_third = 2.0315

N_X, N_CORE, N_Y, N_Z = 4, 2, 4, 4
PAD = 48
BF = jnp.bfloat16
F32 = jnp.float32


def row_perm(dx, flip):
    return [
        (x * 2 + k, ((x + dx) % 4) * 2 + (k ^ flip)) for x in range(4) for k in range(2)
    ]


def col_perm(dy, dz):
    return [
        (y * 4 + z, ((y + dy) % 4) * 4 + (z + dz) % 4) for y in range(4) for z in range(4)
    ]


def send_x(a, d):
    return lax.ppermute(a, "row", row_perm(d, 0))


def swap_core(a):
    return lax.ppermute(a, "row", row_perm(0, 1))


def send_y(a, d):
    return lax.ppermute(a, "col", col_perm(d, 0))


def send_z(a, d):
    return lax.ppermute(a, "col", col_perm(0, d))


def sync(*arrays):
    return lax.optimization_barrier(arrays)


def pick(a, index, axis):
    return lax.dynamic_index_in_dim(a, index % 4, axis=axis, keepdims=False)


def exchange(parts, send, index, axis):
    def to(shift):
        return send(jnp.stack([pick(p, index + shift, axis) for p in parts], axis=0), shift)

    return [to(1), to(-1), to(2)]


def own_stack(parts, index, axis):
    return jnp.stack([pick(p, index, axis) for p in parts], axis=0)


def total(arrays):
    return sum(v.astype(F32) for v in arrays).astype(BF)


def scatter_round(parts_y, parts_z, y, z, *others):
    from_y = exchange(parts_y, send_y, y, 0)
    from_z = exchange(parts_z, send_z, z, 1)
    done = sync(*from_y, *from_z, *others)
    sum_y = total([own_stack(parts_y, y, 0), *done[:3]])
    sum_z = total([own_stack(parts_z, z, 1), *done[3:6]])
    return sum_y, sum_z, done[6:]


def straight(a, send):
    return [send(a, 1), send(a, -1), send(a, 2)]


def plane_gather(a, b, *others):
    first = sync(*straight(a, send_z), *straight(b, send_y), *others)
    a_z = jnp.concatenate([a, *first[:3]], axis=0)
    b_y = jnp.concatenate([b, *first[3:6]], axis=0)
    half = a_z.shape[0] // 2
    plus_a, minus_a, plus_b, minus_b = sync(
        send_y(a_z, 1), send_y(a_z, -1), send_z(b_y, 1), send_z(b_y, -1)
    )
    far = sync(
        send_y(plus_a[:half], 1),
        send_y(minus_a[half:], -1),
        send_z(plus_b[:half], 1),
        send_z(minus_b[half:], -1),
    )
    far_a, far_b = jnp.concatenate(far[:2], axis=0), jnp.concatenate(far[2:], axis=0)
    return [a_z, plus_a, minus_a, far_a], [b_y, plus_b, minus_b, far_b], first[6:]


def regroup_kernel(cols_ref, order_ref, *refs):
    blocks, (low, high) = refs[:8], refs[8:]
    for i in range(8):
        place = order_ref[i]

        @pl.when(place < 4)
        def _():
            low[0, place] = blocks[i][0]

        @pl.when(place >= 4)
        def _():
            high[0, place - 4] = blocks[i][0]


def regroup(blocks, cols, order):
    count, rows, width = blocks[0].shape
    spec = pl.BlockSpec((1, rows, width), lambda j, c, o: (c[j], 0, 0))
    low_spec = pl.BlockSpec((1, 4, rows, width), lambda j, c, o: (j, 0, 0, 0))
    high_spec = pl.BlockSpec((1, 4, rows, width), lambda j, c, o: (j % 4 * 4 + j // 4, 0, 0, 0))
    shape = jax.ShapeDtypeStruct((count, 4, rows, width), blocks[0].dtype)
    return pl.pallas_call(
        regroup_kernel,
        grid_spec=pltpu.PrefetchScalarGridSpec(
            num_scalar_prefetch=2,
            grid=(count,),
            in_specs=[spec] * 8,
            out_specs=[low_spec, high_spec],
        ),
        out_shape=[shape, shape],
        compiler_params=pltpu.CompilerParams(vmem_limit_bytes=32 * 1024 * 1024),
        cost_estimate=pl.CostEstimate(
            flops=0, bytes_accessed=4 * 8 * count * rows * width, transcendentals=0
        ),
    )(cols, order, *blocks)


def positions(match):
    return jnp.cumsum(match, axis=-1) - 1


def selector(target, group):
    match = (target == group).astype(jnp.int32)
    slot = lax.broadcasted_iota(jnp.int32, (PAD, 1), 0)
    return ((positions(match)[None, :] == slot) & (match[None, :] == 1)).astype(BF)


def body(iterate, route):
    rows, wide = iterate.shape
    groups, count, capacity = 8, 16, 42
    q = rows // groups
    width = wide // 2
    scale = 1.0 / (wide * groups)
    block = count * q
    ri, ci = lax.axis_index("row"), lax.axis_index("col")
    x, core, y, z = ri // 2, ri % 2, ci // 4, ci % 4
    flip = core == 1

    parts = iterate.reshape(groups, q, 2, width).transpose(0, 2, 1, 3)
    parts = lax.all_to_all(parts, "row", 0, 0, tiled=True).reshape(count, q, width)
    own = lax.all_to_all(parts, "col", 0, 0, tiled=True).reshape(block, width)
    own, route = sync(own, route)

    def gram(panel):
        part = lax.dot_general(
            panel, own, (((1,), (1,)), ((), ())), preferred_element_type=F32
        )
        return (part * scale).astype(BF).reshape(4, 4, q, block)

    plus, minus = send_x(own, 1), send_x(own, -1)
    sibling = swap_core(own)
    by_z = route.reshape(1, rows)
    by_z = jnp.stack([by_z, *straight(by_z, send_z)], axis=1)
    targets = jnp.stack([by_z, *straight(by_z, send_y)], axis=0).reshape(count, rows)
    sum_y0, sum_z0, (plus, minus, targets) = scatter_round(
        [gram(own)], [gram(sibling)], y, z, plus, minus, targets
    )
    far = [send_x(plus[: block // 2], 1), send_x(minus[block // 2 :], -1)]
    plus_s, minus_s = swap_core(plus), swap_core(minus)
    sum_y1, sum_z1, far = scatter_round(
        [gram(plus), gram(minus)], [gram(plus_s), gram(minus_s)], y, z, *far
    )
    far = jnp.concatenate(far, axis=0)
    far_s = swap_core(far)
    sum_y2, sum_z2, _ = scatter_round([gram(far)], [gram(far_s)], y, z)
    share_s, share_o, _ = scatter_round(
        [jnp.concatenate([sum_z0, sum_z1, sum_z2], axis=0).swapaxes(0, 1)],
        [jnp.concatenate([sum_y0, sum_y1, sum_y2], axis=0)],
        y,
        z,
    )
    share_s, share_o = share_s[0], share_o[0]
    even, odd = jnp.where(flip, share_s, share_o), jnp.where(flip, share_o, share_s)
    ordered = []
    for t in range(4):
        away = (x - t) % 4
        away = away ^ (away >> 1)
        ordered += [pick(even, away, 0), pick(odd, away, 0)]
    gram_share = jnp.stack(ordered, axis=0).reshape(rows, block)

    choose = jnp.concatenate([selector(route[:, 0], g) for g in range(groups)], axis=0)
    routed = jnp.dot(choose, gram_share, preferred_element_type=F32).astype(BF)
    routed = routed.reshape(4, 2, PAD, block)
    other = swap_core(jnp.where(flip, routed[:, 0], routed[:, 1]))
    routed = jnp.stack([jnp.where(flip, routed[:, 1], routed[:, 0]), other], axis=1)
    arrived = sync(*exchange([routed], send_x, x, 0))
    lanes = [v[b] for v in (pick(routed, x, 0), *[v[0] for v in arrived]) for b in range(2)]
    panels = [own, sibling, plus, plus_s, minus, minus_s, far, far_s]

    gram_same = [gram_share, *straight(gram_share, send_x)]
    chunks_a, chunks_b, tied = plane_gather(
        jnp.concatenate(lanes[:4], axis=1),
        jnp.concatenate(lanes[4:], axis=1),
        *panels,
        targets,
        *gram_same,
    )
    panels, targets, gram_same = tied[:8], tied[8], tied[9:]
    gram_blocks = [v for s in gram_same for v in (s, swap_core(s))]
    gram_a = jnp.concatenate(gram_blocks[:4], axis=1)
    gram_b = jnp.concatenate(gram_blocks[4:], axis=1)

    steps = jnp.asarray([0, 1, 3, 2], jnp.int32)
    order = jnp.stack([((x - d) % 4) * 2 + (core ^ b) for d in (0, 1, 3, 2) for b in range(2)])
    sources = (((y - steps) % 4)[:, None] * 4 + ((z - steps) % 4)[None, :]).reshape(count)
    match = (targets == ri).astype(jnp.int32)
    slot_of = jnp.where(match == 1, sources[:, None] * capacity + positions(match), -1)
    slot_of = slot_of.reshape(count, groups, q)
    slots = capacity * count
    slot = lax.broadcasted_iota(jnp.int32, (slots, 1), 0)

    def places(indices):
        return (slot == indices.reshape(1, -1)).astype(BF)

    by_panel = jnp.zeros_like(slot_of).at[sources].set(slot_of)
    by_panel = jnp.take(by_panel, order, axis=1).swapaxes(0, 1)
    rows_rows = (((1,), (1,)), ((), ()))
    gram_cols = lax.dot_general(
        gram_a, places(by_panel[:4]), rows_rows, preferred_element_type=F32
    )
    gram_cols = gram_cols + lax.dot_general(
        gram_b, places(by_panel[4:]), rows_rows, preferred_element_type=F32
    )
    gram_cols = gram_cols.astype(BF).astype(F32)
    flat = [v.reshape(count, q, width) for v in panels]
    low, high = regroup(flat, sources, order)
    half = rows // 2
    low = low.reshape(count * half, width)
    high = high.reshape(count * half, width)
    place_low = places(slot_of[:, :4])
    place_high = places(slot_of[:, 4:].reshape(4, 4, 4, q).swapaxes(0, 1))
    update = jnp.dot(place_low, low, preferred_element_type=F32)
    update = update + jnp.dot(place_high, high, preferred_element_type=F32)
    update = coef_first * update

    source, position = slot // capacity, slot % capacity
    away_y, away_z = (y - source // 4) % 4, (z - source % 4) % 4
    away_y, away_z = away_y ^ (away_y >> 1), away_z ^ (away_z >> 1)
    padded = lax.broadcasted_iota(jnp.int32, (1, count * PAD), 1)
    square = 0.0
    for chunks, gram_rows, column in (
        (chunks_a, gram_a, (away_y * 4 + away_z) * PAD + position),
        (chunks_b, gram_b, (away_z * 4 + away_y) * PAD + position),
    ):
        terms = [
            lax.dot_general(v, gram_rows, rows_rows, preferred_element_type=F32).astype(BF)
            for v in chunks
        ]
        compact = (padded == column).astype(BF)
        square = square + lax.dot_general(
            jnp.concatenate(terms, axis=0),
            compact,
            (((0,), (1,)), ((), ())),
            preferred_element_type=F32,
        )
    square = square.astype(BF).astype(F32)
    mixer = (coef_second * gram_cols + coef_third * square).astype(BF)
    mixer_a, mixer_b, (update,) = plane_gather(mixer[:half], mixer[half:], update)

    near = 3 * 4 * half
    for chunks, panel in (
        (jnp.concatenate(mixer_a[:3], axis=0), low[:near]),
        (jnp.concatenate(mixer_b[:3], axis=0), high[:near]),
        (mixer_a[3], low[near:]),
        (mixer_b[3], high[near:]),
    ):
        (update,) = sync(update)
        update = update + lax.dot_general(
            chunks, panel, (((0,), (0,)), ((), ())), preferred_element_type=F32
        )
    return update.astype(BF)


def solution(mesh):
    in_specs = (P("col", "row"), P("col", None))
    out_specs = P("row", "col")
    return jax.shard_map(body, mesh=mesh, in_specs=in_specs, out_specs=out_specs, check_vma=False)
```

```python
import jax
import jax.numpy as jnp
from jax import lax
from jax.experimental import pallas as pl
from jax.experimental.pallas import tpu as pltpu
from jax.sharding import PartitionSpec as P

coef_first = 3.4445
coef_second = -4.775
coef_third = 2.0315

N_X, N_CORE, N_Y, N_Z = 4, 2, 4, 4
PAD = 48
BF = jnp.bfloat16
F32 = jnp.float32


def moved(dx, flip, dy, dz):
    pairs = []
    for x in range(4):
        for k in range(2):
            for y in range(4):
                for z in range(4):
                    to_row = ((x + dx) % 4) * 2 + (k ^ flip)
                    to_col = ((y + dy[k]) % 4) * 4 + (z + dz[k]) % 4
                    pairs.append(((x * 2 + k) * 16 + y * 4 + z, to_row * 16 + to_col))
    return pairs


def send(a, pairs):
    return lax.ppermute(a, ("row", "col"), pairs)


def send_x(a, d):
    return send(a, moved(d, 0, (0, 0), (0, 0)))


def swap_core(a):
    return send(a, moved(0, 1, (0, 0), (0, 0)))


def send_first(a, d):
    return send(a, moved(0, 0, (d, 0), (0, d)))


def send_second(a, d):
    return send(a, moved(0, 0, (0, d), (d, 0)))


def sync(*arrays):
    return lax.optimization_barrier(arrays)


def pick(a, index, axis):
    return lax.dynamic_index_in_dim(a, index % 4, axis=axis, keepdims=False)


def straight(a, move):
    return [move(a, 1), move(a, -1), move(a, 2)]


def total(arrays):
    return sum(v.astype(F32) for v in arrays).astype(BF)


def halves(plus, minus, move):
    half = plus.shape[0] // 2
    return [move(plus[:half], 1), move(minus[half:], -1)]


def regroup_kernel(cols_ref, order_ref, *refs):
    blocks, (near, far) = refs[:8], refs[8:]
    step = pl.program_id(0)

    @pl.when(step < 12)
    def _():
        for i in range(8):
            near[0, order_ref[i]] = blocks[i][0]

    @pl.when(step >= 12)
    def _():
        for i in range(8):
            far[0, order_ref[i]] = blocks[i][0]


def regroup(blocks, cols, order):
    count, rows, width = blocks[0].shape
    spec = pl.BlockSpec((1, rows, width), lambda j, c, o: (c[j], 0, 0))
    near_spec = pl.BlockSpec((1, 8, rows, width), lambda j, c, o: (jnp.minimum(j, 11), 0, 0, 0))
    far_spec = pl.BlockSpec((1, 8, rows, width), lambda j, c, o: (jnp.maximum(j - 12, 0), 0, 0, 0))
    return pl.pallas_call(
        regroup_kernel,
        grid_spec=pltpu.PrefetchScalarGridSpec(
            num_scalar_prefetch=2,
            grid=(count,),
            in_specs=[spec] * 8,
            out_specs=[near_spec, far_spec],
        ),
        out_shape=[
            jax.ShapeDtypeStruct((n, 8, rows, width), blocks[0].dtype) for n in (12, 4)
        ],
        compiler_params=pltpu.CompilerParams(vmem_limit_bytes=32 * 1024 * 1024),
        cost_estimate=pl.CostEstimate(
            flops=0, bytes_accessed=4 * 8 * count * rows * width, transcendentals=0
        ),
    )(cols, order, *blocks)


def positions(match):
    return jnp.cumsum(match, axis=-1) - 1


def selector(target, group):
    match = (target == group).astype(jnp.int32)
    slot = lax.broadcasted_iota(jnp.int32, (PAD, 1), 0)
    return ((positions(match)[None, :] == slot) & (match[None, :] == 1)).astype(BF)


def body(iterate, route):
    rows, wide = iterate.shape
    groups, count, capacity = 8, 16, 42
    q = rows // groups
    width = wide // 2
    scale = 1.0 / (wide * groups)
    block = count * q
    ri, ci = lax.axis_index("row"), lax.axis_index("col")
    x, core, y, z = ri // 2, ri % 2, ci // 4, ci % 4
    flip = core == 1
    first, second = jnp.where(flip, z, y), jnp.where(flip, y, z)
    rows_rows = (((1,), (1,)), ((), ()))

    parts = iterate.reshape(groups, q, 2, width).transpose(0, 2, 1, 3)
    parts = lax.all_to_all(parts, "row", 0, 0, tiled=True).reshape(count, q, width)
    own = lax.all_to_all(parts, "col", 0, 0, tiled=True).reshape(block, width)
    own, route = sync(own, route)

    def gram(panel):
        part = lax.dot_general(panel, own, rows_rows, preferred_element_type=F32)
        return (part * scale).astype(BF).reshape(4, 4, q, block)

    def pick_first(parts, index):
        return jnp.stack(
            [jnp.where(flip, pick(p, index, 1), pick(p, index, 0)) for p in parts], axis=0
        )

    def scatter_first(parts):
        return [send_first(pick_first(parts, first + d), d) for d in (1, -1, 2)]

    plus, minus = send_x(own, 1), send_x(own, -1)
    sibling = swap_core(own)
    grams = [gram(own), gram(sibling)]
    *got, plus, minus = sync(*scatter_first(grams), plus, minus)
    sums = [total([pick_first(grams, first), *got])]

    swaps = sync(swap_core(plus), swap_core(minus))
    far = halves(plus, minus, send_x)
    grams = [gram(plus), gram(swaps[0]), gram(minus), gram(swaps[1])]
    *got, far_a, far_b = sync(*scatter_first(grams), *far)
    sums.append(total([pick_first(grams, first), *got]))

    far = jnp.concatenate([far_a, far_b], axis=0)
    far_s = swap_core(far)
    grams = [gram(far), gram(far_s)]
    got = sync(*scatter_first(grams))
    sums.append(total([pick_first(grams, first), *got]))
    panels = [own, sibling, plus, swaps[0], minus, swaps[1], far, far_s]

    sums = jnp.concatenate(sums, axis=0)
    sums, route, *panels = sync(sums, route, *panels)
    got = [send_second(pick(sums, second + d, 1), d) for d in (1, -1, 2)]

    steps = jnp.asarray([0, 1, 3, 2], jnp.int32)
    first_of, second_of = (first - steps) % 4, (second - steps) % 4
    sources = jnp.where(
        flip,
        second_of[:, None] * 4 + first_of[None, :],
        first_of[None, :] * 4 + second_of[:, None],
    ).reshape(count)
    order = jnp.stack([((x - d) % 4) * 2 + (core ^ b) for d in (0, 1, 3, 2) for b in range(2)])
    near, away = regroup([v.reshape(count, q, width) for v in panels], sources, order)
    *got, near, away = sync(*got, near, away)
    share = total([pick(sums, second, 1), *got])
    ordered = []
    for t in range(4):
        d = (x - t) % 4
        d = d ^ (d >> 1)
        for k in range(2):
            ordered.append(lax.dynamic_index_in_dim(share, d * 2 + (core ^ k), 0, keepdims=False))
    gram_share = jnp.concatenate(ordered, axis=0)

    choose = jnp.concatenate([selector(route[:, 0], g) for g in range(groups)], axis=0)
    routed = jnp.dot(choose, gram_share, preferred_element_type=F32).astype(BF)
    routed = routed.reshape(4, 2, PAD, block)
    other = swap_core(jnp.where(flip, routed[:, 0], routed[:, 1]))
    routed = jnp.stack([jnp.where(flip, routed[:, 1], routed[:, 0]), other], axis=1)
    arrived = sync(*[send_x(pick(routed, x + d, 0), d) for d in (1, -1, 2)], gram_share)
    lanes = [v[b] for v in (pick(routed, x, 0), *arrived[:3]) for b in range(2)]
    lanes = jnp.concatenate(lanes, axis=1)
    lanes, gram_share, near, away, route = sync(lanes, arrived[3], near, away, route)

    got = straight(lanes, send_first)
    by_first = route.reshape(1, rows)
    by_first = jnp.stack([by_first, *straight(by_first, send_first)], axis=1)
    targets = jnp.stack([by_first, *straight(by_first, send_second)], axis=0)
    targets = targets.reshape(count, rows)
    match = (targets == ri).astype(jnp.int32)
    slot_of = jnp.where(match == 1, sources[:, None] * capacity + positions(match), -1)
    slots = capacity * count
    slot = lax.broadcasted_iota(jnp.int32, (slots, 1), 0)

    def places(indices):
        return (slot == indices.reshape(1, -1)).astype(BF)

    got = sync(*got, slot_of)
    slot_of = got[3]
    lanes = jnp.concatenate([lanes, *got[:3]], axis=0)
    lanes, slot_of, gram_share = sync(lanes, slot_of, gram_share)

    got = [send_second(lanes, 1), send_second(lanes, -1)]
    gram_near = [gram_share, send_x(gram_share, 1), send_x(gram_share, -1)]
    gram_near = jnp.stack(gram_near, axis=0)
    gram_far = send_x(gram_share, 2)
    near = near.reshape(12 * rows, width)
    away = away.reshape(4 * rows, width)
    update = jnp.dot(places(slot_of[:12]), near, preferred_element_type=F32)
    (update,) = sync(update)
    update = update + jnp.dot(places(slot_of[12:]), away, preferred_element_type=F32)
    update = coef_first * update
    gram_near_s, gram_far_s = swap_core(gram_near), swap_core(gram_far)
    gram_rows = jnp.concatenate(
        [v for d in range(3) for v in (gram_near[d], gram_near_s[d])] + [gram_far, gram_far_s],
        axis=1,
    )
    plus, minus, update, gram_rows = sync(*got, update, gram_rows)

    def square_rows(chunk):
        term = lax.dot_general(chunk, gram_rows, rows_rows, preferred_element_type=F32)
        return term.astype(BF)

    far = halves(plus, minus, send_second)
    by_panel = jnp.zeros_like(slot_of).at[sources].set(slot_of).reshape(count, groups, q)
    by_panel = jnp.take(by_panel, order, axis=1).swapaxes(0, 1)
    gram_cols = lax.dot_general(
        gram_rows, places(by_panel), rows_rows, preferred_element_type=F32
    ).astype(BF)
    terms = [square_rows(v) for v in (lanes, plus, minus)]
    *far, gram_cols, t0, t1, t2 = sync(*far, gram_cols, *terms)
    terms = [t0, t1, t2, square_rows(jnp.concatenate(far, axis=0))]

    source, position = slot // capacity, slot % capacity
    source_y, source_z = source // 4, source % 4
    away_first = (first - jnp.where(flip, source_z, source_y)) % 4
    away_second = (second - jnp.where(flip, source_y, source_z)) % 4
    away_first, away_second = away_first ^ (away_first >> 1), away_second ^ (away_second >> 1)
    column = (away_second * 4 + away_first) * PAD + position
    compact = (lax.broadcasted_iota(jnp.int32, (1, count * PAD), 1) == column).astype(BF)
    square = lax.dot_general(
        jnp.concatenate(terms, axis=0),
        compact,
        (((0,), (1,)), ((), ())),
        preferred_element_type=F32,
    )
    square = square.astype(BF).astype(F32)
    mixer = (coef_second * gram_cols.astype(F32) + coef_third * square).astype(BF)

    def product(chunk, panel):
        return lax.dot_general(
            chunk, panel, (((0,), (0,)), ((), ())), preferred_element_type=F32
        )

    got = sync(*straight(mixer, send_first))
    mixer = jnp.concatenate([mixer, *got], axis=0)
    (mixer,) = sync(mixer)
    plus, minus = send_second(mixer, 1), send_second(mixer, -1)
    near = near.reshape(3, 4 * rows, width)
    update = update + product(mixer, near[0])
    plus, minus, update = sync(plus, minus, update)
    far = halves(plus, minus, send_second)
    update = update + product(plus, near[1])
    (update,) = sync(update)
    update = update + product(minus, near[2])
    *far, update = sync(*far, update)
    update = update + product(jnp.concatenate(far, axis=0), away)
    return update.astype(BF)


def solution(mesh):
    in_specs = (P("col", "row"), P("col", None))
    out_specs = P("row", "col")
    return jax.shard_map(body, mesh=mesh, in_specs=in_specs, out_specs=out_specs, check_vma=False)
```

```python
import jax
import jax.numpy as jnp
from jax import lax
from jax.experimental import pallas as pl
from jax.experimental.pallas import tpu as pltpu
from jax.sharding import PartitionSpec as P

coef_first = 3.4445
coef_second = -4.775
coef_third = 2.0315

N_X, N_CORE, N_Y, N_Z = 4, 2, 4, 4
PAD = 48
BF = jnp.bfloat16
F32 = jnp.float32


def moved(dx, flip, dy, dz):
    pairs = []
    for x in range(4):
        for k in range(2):
            for y in range(4):
                for z in range(4):
                    to_row = ((x + dx) % 4) * 2 + (k ^ flip)
                    to_col = ((y + dy[k]) % 4) * 4 + (z + dz[k]) % 4
                    pairs.append(((x * 2 + k) * 16 + y * 4 + z, to_row * 16 + to_col))
    return pairs


def send(a, pairs):
    return lax.ppermute(a, ("row", "col"), pairs)


def send_x(a, d):
    return send(a, moved(d, 0, (0, 0), (0, 0)))


def swap_core(a):
    return send(a, moved(0, 1, (0, 0), (0, 0)))


def send_first(a, d):
    return send(a, moved(0, 0, (d, 0), (0, d)))


def send_second(a, d):
    return send(a, moved(0, 0, (0, d), (d, 0)))


def sync(*arrays):
    return lax.optimization_barrier(arrays)


def pick(a, index, axis):
    return lax.dynamic_index_in_dim(a, index % 4, axis=axis, keepdims=False)


def straight(a, move):
    return [move(a, 1), move(a, -1), move(a, 2)]


def total(arrays):
    return sum(v.astype(F32) for v in arrays).astype(BF)


def halves(plus, minus, move):
    half = plus.shape[0] // 2
    return [move(plus[:half], 1), move(minus[half:], -1)]


def regroup_kernel(cols_ref, order_ref, *refs):
    blocks, (near, far) = refs[:8], refs[8:]
    step = pl.program_id(0)

    @pl.when(step < 12)
    def _():
        for i in range(8):
            near[0, order_ref[i]] = blocks[i][0]

    @pl.when(step >= 12)
    def _():
        for i in range(8):
            far[0, order_ref[i]] = blocks[i][0]


def regroup(blocks, cols, order):
    count, rows, width = blocks[0].shape
    spec = pl.BlockSpec((1, rows, width), lambda j, c, o: (c[j], 0, 0))
    near_spec = pl.BlockSpec((1, 8, rows, width), lambda j, c, o: (jnp.minimum(j, 11), 0, 0, 0))
    far_spec = pl.BlockSpec((1, 8, rows, width), lambda j, c, o: (jnp.maximum(j - 12, 0), 0, 0, 0))
    return pl.pallas_call(
        regroup_kernel,
        grid_spec=pltpu.PrefetchScalarGridSpec(
            num_scalar_prefetch=2,
            grid=(count,),
            in_specs=[spec] * 8,
            out_specs=[near_spec, far_spec],
        ),
        out_shape=[
            jax.ShapeDtypeStruct((n, 8, rows, width), blocks[0].dtype) for n in (12, 4)
        ],
        compiler_params=pltpu.CompilerParams(vmem_limit_bytes=32 * 1024 * 1024),
        cost_estimate=pl.CostEstimate(
            flops=0, bytes_accessed=4 * 8 * count * rows * width, transcendentals=0
        ),
    )(cols, order, *blocks)


def positions(match):
    return jnp.cumsum(match, axis=-1) - 1


def body(iterate, route):
    rows, wide = iterate.shape
    groups, count, capacity = 8, 16, 42
    q = rows // groups
    width = wide // 2
    scale = 1.0 / (wide * groups)
    block = count * q
    ri, ci = lax.axis_index("row"), lax.axis_index("col")
    x, core, y, z = ri // 2, ri % 2, ci // 4, ci % 4
    flip = core == 1
    first, second = jnp.where(flip, z, y), jnp.where(flip, y, z)
    rows_rows = (((1,), (1,)), ((), ()))

    parts = iterate.reshape(groups, q, 2, width).transpose(0, 2, 1, 3)
    parts = lax.all_to_all(parts, "row", 0, 0, tiled=True).reshape(count, q, width)
    own = lax.all_to_all(parts, "col", 0, 0, tiled=True).reshape(block, width)
    own, route = sync(own, route)

    def gram(panel):
        part = lax.dot_general(panel, own, rows_rows, preferred_element_type=F32)
        return (part * scale).astype(BF).reshape(4, 4, q, block)

    def pick_first(parts, index, axis):
        return jnp.stack(
            [jnp.where(flip, pick(p, index, 1 - axis), pick(p, index, axis)) for p in parts], axis=0
        )

    def scatter_first(parts):
        return [send_first(pick_first(parts, first + d, 0), d) for d in (1, -1, 2)]

    def gathered(parts, got):
        return total([pick_first(parts, first, 0), *got])

    steps = jnp.asarray([0, 1, 3, 2], jnp.int32)
    order = jnp.stack([((x - d) % 4) * 2 + (core ^ b) for d in (0, 1, 3, 2) for b in range(2)])
    first_of, second_of = (first - steps) % 4, (second - steps) % 4
    sources = jnp.where(
        flip,
        second_of[:, None] * 4 + first_of[None, :],
        first_of[None, :] * 4 + second_of[:, None],
    ).reshape(count)
    slots = capacity * count
    slot = lax.broadcasted_iota(jnp.int32, (slots, 1), 0)

    plus, minus = send_x(own, 1), send_x(own, -1)
    sibling = swap_core(own)
    grams = [gram(own), gram(sibling)]
    *got, route, own_x, sibling_x = sync(*scatter_first(grams), route, own, sibling)
    sum_0 = gathered(grams, got)

    by_first = route.reshape(1, rows)
    by_first = jnp.stack([by_first, *straight(by_first, send_first)], axis=1)
    targets = jnp.stack([by_first, *straight(by_first, send_second)], axis=0)
    targets = targets.reshape(count, rows)
    match = (targets == ri).astype(jnp.int32)
    slot_of = jnp.where(match == 1, sources[:, None] * capacity + positions(match), -1)
    by_panel = jnp.zeros_like(slot_of).at[sources].set(slot_of).reshape(count, groups, q)
    by_panel = jnp.take(by_panel, order, axis=1).swapaxes(0, 1).reshape(groups, block)
    labels = lax.broadcasted_iota(jnp.int32, (groups, 1), 0)
    match = (route.reshape(1, rows) == labels).astype(jnp.int32)
    row_slot = jnp.sum(match * (labels * PAD + positions(match)), axis=0)
    row_slot = jnp.take(row_slot.reshape(groups, q), order, axis=0).reshape(1, rows)
    choose = (lax.broadcasted_iota(jnp.int32, (groups * PAD, 1), 0) == row_slot).astype(BF)

    def placed(i, panel):
        place = (slot == by_panel[i].reshape(1, block)).astype(BF)
        return jnp.dot(place, panel, preferred_element_type=F32)

    update = placed(0, own_x)
    (update,) = sync(update)
    update = update + placed(1, sibling_x)
    plus, minus, update, by_panel, choose = sync(plus, minus, update, by_panel, choose)

    plus_s, minus_s = swap_core(plus), swap_core(minus)
    far = halves(plus, minus, send_x)
    grams = [gram(plus), gram(minus)]
    *got, update, plus_x, minus_x = sync(*scatter_first(grams), update, plus, minus)
    sum_1 = gathered(grams, got)
    update = update + placed(2, plus_x)
    (update,) = sync(update)
    update = update + placed(4, minus_x)
    grams = [gram(plus_s), gram(minus_s)]
    *got, far_a, far_b, update = sync(*scatter_first(grams), *far, update)
    sum_2 = gathered(grams, got)

    far = jnp.concatenate([far_a, far_b], axis=0)
    far_s = swap_core(far)
    grams = [gram(far)]
    *got, update, far_x, plus_x = sync(*scatter_first(grams), update, far, plus_s)
    sum_3 = gathered(grams, got)
    grams = [gram(far_s)]
    update = update + placed(6, far_x)
    (update,) = sync(update)
    update = update + placed(3, plus_x)
    *got, update = sync(*scatter_first(grams), update)
    sum_4 = gathered(grams, got)

    sums = [sum_0, sum_1[:1], sum_2[:1], sum_1[1:], sum_2[1:], sum_3, sum_4]
    sums = jnp.concatenate(sums, axis=0)
    sums, update, minus_x, far_x = sync(sums, update, minus_s, far_s)
    got = [send_second(pick(sums, second + d, 1), d) for d in (1, -1, 2)]
    update = update + placed(5, minus_x)
    (update,) = sync(update)
    update = update + placed(7, far_x)
    *got, update = sync(*got, update)
    share = total([pick(sums, second, 1), *got])

    routed = jnp.dot(choose, share.reshape(rows, block), preferred_element_type=F32).astype(BF)
    routed = routed.reshape(4, 2, PAD, block)
    other = swap_core(jnp.where(flip, routed[:, 0], routed[:, 1]))
    routed = jnp.stack([jnp.where(flip, routed[:, 1], routed[:, 0]), other], axis=1)
    *got, share = sync(*[send_x(pick(routed, x + d, 0), d) for d in (1, -1, 2)], share)
    lanes = [v[b] for v in (pick(routed, x, 0), *got) for b in range(2)]
    lanes = jnp.concatenate(lanes, axis=1)

    lanes, share = sync(lanes, share)
    got = straight(lanes, send_first)
    ordered = []
    for t in range(4):
        d = (x - t) % 4
        d = d ^ (d >> 1)
        for k in range(2):
            ordered.append(lax.dynamic_index_in_dim(share, d * 2 + (core ^ k), 0, keepdims=False))
    gram_share = jnp.concatenate(ordered, axis=0)
    *got, gram_share = sync(*got, gram_share)

    top, low = jnp.concatenate([lanes, got[0]], axis=0), jnp.concatenate(got[1:], axis=0)
    panels = [own, sibling, plus, plus_s, minus, minus_s, far, far_s]
    top, low, gram_share, *panels = sync(top, low, gram_share, *panels)
    plus_t, minus_l = send_second(top, 1), send_second(low, -1)
    gram_p, gram_m = send_x(gram_share, 1), send_x(gram_share, -1)
    gram_s = swap_core(gram_share)
    near, away = regroup([v.reshape(count, q, width) for v in panels], sources, order)
    plus_t, minus_l, gram_p, gram_m, gram_s, near, away = sync(
        plus_t, minus_l, gram_p, gram_m, gram_s, near, away
    )
    gram_f = send_x(gram_share, 2)
    plus_l, minus_t = send_second(low, 1), send_second(top, -1)
    far_t, far_l = send_second(plus_t, 1), send_second(minus_l, -1)
    gram_ps, gram_ms, gram_fs = swap_core(gram_p), swap_core(gram_m), swap_core(gram_f)
    gram_rows = jnp.concatenate(
        [gram_share, gram_s, gram_p, gram_ps, gram_m, gram_ms, gram_f, gram_fs], axis=1
    )
    place = (slot == by_panel.reshape(1, groups * block)).astype(BF)
    gram_cols = lax.dot_general(gram_rows, place, rows_rows, preferred_element_type=F32)
    gram_cols = gram_cols.astype(BF)

    def square_rows(chunk):
        term = lax.dot_general(chunk, gram_rows, rows_rows, preferred_element_type=F32)
        return term.astype(BF)

    terms = [square_rows(v) for v in (top, low, plus_t, plus_l, minus_t, minus_l)]
    far_t, far_l, gram_cols, gram_rows, *terms = sync(far_t, far_l, gram_cols, gram_rows, *terms)
    terms.append(square_rows(jnp.concatenate([far_t, far_l], axis=0)))

    source, position = slot // capacity, slot % capacity
    source_y, source_z = source // 4, source % 4
    away_first = (first - jnp.where(flip, source_z, source_y)) % 4
    away_second = (second - jnp.where(flip, source_y, source_z)) % 4
    away_first, away_second = away_first ^ (away_first >> 1), away_second ^ (away_second >> 1)
    column = (away_second * 4 + away_first) * PAD + position
    compact = (lax.broadcasted_iota(jnp.int32, (1, count * PAD), 1) == column).astype(BF)
    square = lax.dot_general(
        jnp.concatenate(terms, axis=0),
        compact,
        (((0,), (1,)), ((), ())),
        preferred_element_type=F32,
    )
    square = square.astype(BF).astype(F32)
    mixer = (coef_second * gram_cols.astype(F32) + coef_third * square).astype(BF)

    near = near.reshape(6, 2 * rows, width)

    def product(chunk, panel):
        return lax.dot_general(
            chunk, panel, (((0,), (0,)), ((), ())), preferred_element_type=F32
        )

    got = sync(*straight(mixer, send_first))
    top, low = jnp.concatenate([mixer, got[0]], axis=0), jnp.concatenate(got[1:], axis=0)
    top, low = sync(top, low)
    plus_t, minus_l = send_second(top, 1), send_second(low, -1)
    plus_t, minus_l, own_t, own_l = sync(plus_t, minus_l, top, low)
    plus_l, minus_t = send_second(low, 1), send_second(top, -1)
    far_t, far_l = send_second(plus_t, 1), send_second(minus_l, -1)
    update = coef_first * update + product(own_t, near[0])
    for chunk, panel in ((own_l, near[1]), (plus_t, near[2]), (minus_l, near[5])):
        (update,) = sync(update)
        update = update + product(chunk, panel)
    plus_l, minus_t, update = sync(plus_l, minus_t, update)
    update = update + product(plus_l, near[3])
    (update,) = sync(update)
    update = update + product(minus_t, near[4])
    far_t, far_l, update = sync(far_t, far_l, update)
    update = update + product(jnp.concatenate([far_t, far_l], axis=0), away.reshape(4 * rows, width))
    return update.astype(BF)


def solution(mesh):
    in_specs = (P("col", "row"), P("col", None))
    out_specs = P("row", "col")
    return jax.shard_map(body, mesh=mesh, in_specs=in_specs, out_specs=out_specs, check_vma=False)
```

```python
import jax
import jax.numpy as jnp
from jax import lax
from jax.experimental import pallas as pl
from jax.experimental.pallas import tpu as pltpu
from jax.sharding import PartitionSpec as P

coef_first = 3.4445
coef_second = -4.775
coef_third = 2.0315

N_X, N_CORE, N_Y, N_Z = 4, 2, 4, 4
PAD = 48
BF = jnp.bfloat16
F32 = jnp.float32


def moved(dx, flip, dy, dz):
    pairs = []
    for x in range(4):
        for k in range(2):
            for y in range(4):
                for z in range(4):
                    to_row = ((x + dx) % 4) * 2 + (k ^ flip)
                    to_col = ((y + dy[k]) % 4) * 4 + (z + dz[k]) % 4
                    pairs.append(((x * 2 + k) * 16 + y * 4 + z, to_row * 16 + to_col))
    return pairs


def send(a, pairs):
    return lax.ppermute(a, ("row", "col"), pairs)


def send_x(a, d):
    return send(a, moved(d, 0, (0, 0), (0, 0)))


def swap_core(a):
    return send(a, moved(0, 1, (0, 0), (0, 0)))


def send_first(a, d):
    return send(a, moved(0, 0, (d, 0), (0, d)))


def send_second(a, d):
    return send(a, moved(0, 0, (0, d), (d, 0)))


def sync(*arrays):
    return lax.optimization_barrier(arrays)


def pick(a, index, axis):
    return lax.dynamic_index_in_dim(a, index % 4, axis=axis, keepdims=False)


def straight(a, move):
    return [move(a, 1), move(a, -1), move(a, 2)]


def total(arrays):
    return sum(v.astype(F32) for v in arrays).astype(BF)


def halves(plus, minus, move):
    half = plus.shape[0] // 2
    return [move(plus[:half], 1), move(minus[half:], -1)]


def regroup_kernel(cols_ref, place_ref, same, sibling, *refs):
    out, core = refs[-1], place_ref[1]
    out[0, core] = same[0]
    out[0, 1 - core] = sibling[0]


def regroup(same, sibling, cols, place, filled=None):
    count, rows, width = same.shape
    spec = pl.BlockSpec((1, rows, width), lambda j, c, o: (c[j], 0, 0))
    out_spec = pl.BlockSpec((1, 2, rows, width), lambda j, c, o: (j, o[0], 0, 0))
    operands, specs, aliases = [same, sibling], [spec, spec], {}
    if filled is not None:
        operands, specs, aliases = [*operands, filled], [*specs, pl.BlockSpec(memory_space=pl.ANY)], {4: 0}
    return pl.pallas_call(
        regroup_kernel,
        grid_spec=pltpu.PrefetchScalarGridSpec(
            num_scalar_prefetch=2,
            grid=(count,),
            in_specs=specs,
            out_specs=out_spec,
        ),
        out_shape=jax.ShapeDtypeStruct((count, 8, rows, width), same.dtype),
        input_output_aliases=aliases,
        compiler_params=pltpu.CompilerParams(vmem_limit_bytes=16 * 1024 * 1024),
        cost_estimate=pl.CostEstimate(
            flops=0, bytes_accessed=8 * count * rows * width, transcendentals=0
        ),
    )(cols, place, *operands)


def positions(match):
    return jnp.cumsum(match, axis=-1) - 1


def body(iterate, route):
    rows, wide = iterate.shape
    groups, count, capacity = 8, 16, 42
    q = rows // groups
    width = wide // 2
    scale = 1.0 / (wide * groups)
    block = count * q
    ri, ci = lax.axis_index("row"), lax.axis_index("col")
    x, core, y, z = ri // 2, ri % 2, ci // 4, ci % 4
    flip = core == 1
    first, second = jnp.where(flip, z, y), jnp.where(flip, y, z)
    rows_rows = (((1,), (1,)), ((), ()))

    parts = iterate.reshape(groups, q, 2, width).transpose(0, 2, 1, 3)
    parts = lax.all_to_all(parts, "row", 0, 0, tiled=True).reshape(count, q, width)
    own = lax.all_to_all(parts, "col", 0, 0, tiled=True).reshape(block, width)
    own, route = sync(own, route)

    def gram(panel):
        part = lax.dot_general(panel, own, rows_rows, preferred_element_type=F32)
        return (part * scale).astype(BF).reshape(4, 4, q, block)

    def pick_first(parts, index, axis):
        return jnp.stack(
            [jnp.where(flip, pick(p, index, 1 - axis), pick(p, index, axis)) for p in parts], axis=0
        )

    def scatter_first(parts):
        return [send_first(pick_first(parts, first + d, 0), d) for d in (1, -1, 2)]

    def gathered(parts, got):
        return total([pick_first(parts, first, 0), *got])

    steps = jnp.asarray([0, 1, 3, 2], jnp.int32)
    order = jnp.stack([((x - d) % 4) * 2 + (core ^ b) for d in (0, 1, 3, 2) for b in range(2)])
    first_of, second_of = (first - steps) % 4, (second - steps) % 4
    sources = jnp.where(
        flip,
        second_of[:, None] * 4 + first_of[None, :],
        first_of[None, :] * 4 + second_of[:, None],
    ).reshape(count)
    slots = capacity * count
    slot = lax.broadcasted_iota(jnp.int32, (slots, 1), 0)

    def grouped(same, sibling, d, filled=None):
        place = jnp.stack([(x - d) % 4, core])
        return regroup(
            same.reshape(count, q, width), sibling.reshape(count, q, width), sources, place, filled
        )

    plus, minus = send_x(own, 1), send_x(own, -1)
    sibling = swap_core(own)
    grams = [gram(own), gram(sibling)]
    by_shard = grouped(own, sibling, 0)
    *got, plus, minus, by_shard = sync(*scatter_first(grams), plus, minus, by_shard)
    sum_0 = gathered(grams, got)

    plus_s, minus_s = swap_core(plus), swap_core(minus)
    far = halves(plus, minus, send_x)
    grams = [gram(plus), gram(minus)]
    plus_s, minus_s, *grams = sync(plus_s, minus_s, *grams)
    got = scatter_first(grams)
    sum_1 = gathered(grams, got)
    grams = [gram(plus_s), gram(minus_s)]
    *got, far_a, far_b = sync(*scatter_first(grams), *far)
    sum_2 = gathered(grams, got)

    far = jnp.concatenate([far_a, far_b], axis=0)
    far_s = swap_core(far)
    grams = [gram(far), gram(far_s)]
    (plus_x, plus_s_x, by_shard, far, far_s) = sync(plus, plus_s, by_shard, far, far_s)
    by_shard = grouped(plus_x, plus_s_x, 1, by_shard)
    *got, by_shard = sync(*scatter_first(grams), by_shard)
    sum_3 = gathered(grams, got)

    sums = [sum_0, sum_1[:1], sum_2[:1], sum_1[1:], sum_2[1:], sum_3]
    sums = jnp.concatenate(sums, axis=0)
    labels = lax.broadcasted_iota(jnp.int32, (groups, 1), 0)
    match = (route.reshape(1, rows) == labels).astype(jnp.int32)
    row_slot = jnp.sum(match * (labels * PAD + positions(match)), axis=0)
    row_slot = jnp.take(row_slot.reshape(groups, q), order, axis=0).reshape(1, rows)
    choose = (lax.broadcasted_iota(jnp.int32, (groups * PAD, 1), 0) == row_slot).astype(BF)
    sums, by_shard, minus_x, minus_s_x = sync(sums, by_shard, minus, minus_s)
    got = [send_second(pick(sums, second + d, 1), d) for d in (1, -1, 2)]
    by_shard = grouped(minus_x, minus_s_x, 3, by_shard)
    *got, by_shard, choose = sync(*got, by_shard, choose)
    share = total([pick(sums, second, 1), *got])

    routed = jnp.dot(choose, share.reshape(rows, block), preferred_element_type=F32).astype(BF)
    routed = routed.reshape(4, 2, PAD, block)
    other = swap_core(jnp.where(flip, routed[:, 0], routed[:, 1]))
    routed = jnp.stack([jnp.where(flip, routed[:, 1], routed[:, 0]), other], axis=1)
    *got, share = sync(*[send_x(pick(routed, x + d, 0), d) for d in (1, -1, 2)], share)
    lanes = [v[b] for v in (pick(routed, x, 0), *got) for b in range(2)]
    lanes = jnp.concatenate(lanes, axis=1)
    mark = jnp.pad(route.reshape(1, rows).astype(BF), ((0, 0), (0, groups * block - rows)))
    is_mark = lax.broadcasted_iota(jnp.int32, (PAD, 1), 0) == capacity
    lanes = jnp.where(is_mark, mark, lanes)

    lanes, share = sync(lanes, share)
    got = straight(lanes, send_first)
    ordered = []
    for t in range(4):
        d = (x - t) % 4
        d = d ^ (d >> 1)
        for k in range(2):
            ordered.append(lax.dynamic_index_in_dim(share, d * 2 + (core ^ k), 0, keepdims=False))
    gram_share = jnp.concatenate(ordered, axis=0)
    *got, gram_share = sync(*got, gram_share)

    top, low = jnp.concatenate([lanes, got[0]], axis=0), jnp.concatenate(got[1:], axis=0)
    top, low, gram_share, by_shard, far, far_s = sync(top, low, gram_share, by_shard, far, far_s)
    plus_t, minus_l = send_second(top, 1), send_second(low, -1)
    gram_p, gram_m = send_x(gram_share, 1), send_x(gram_share, -1)
    gram_s = swap_core(gram_share)
    by_shard = grouped(far, far_s, 2, by_shard)
    plus_t, minus_l, gram_p, gram_m, gram_s, by_shard = sync(
        plus_t, minus_l, gram_p, gram_m, gram_s, by_shard
    )
    gram_f = send_x(gram_share, 2)
    plus_l, minus_t = send_second(low, 1), send_second(top, -1)
    far_t, far_l = send_second(plus_t, 1), send_second(minus_l, -1)
    gram_ps, gram_ms, gram_fs = swap_core(gram_p), swap_core(gram_m), swap_core(gram_f)
    gram_rows = jnp.concatenate(
        [gram_share, gram_s, gram_p, gram_ps, gram_m, gram_ms, gram_f, gram_fs], axis=1
    )

    lane = lax.broadcasted_iota(jnp.int32, (1, groups * block), 1)
    lane_block, lane_c, lane_q = lane // block, lane % block // q, lane % q
    lane_d = lane_block // 2
    lane_d = lane_d ^ (lane_d >> 1)
    lane_s = ((x - lane_d) % 4) * 2 + (core ^ (lane_block % 2))
    lane_row = jnp.where(lane_c == ci, lane_s * q + lane_q, -1)
    unit = (lax.broadcasted_iota(jnp.int32, (rows, 1), 0) == lane_row).astype(BF)
    both = jnp.concatenate([gram_rows, unit], axis=0)

    def mixer_rows(chunk):
        term = lax.dot_general(chunk, both, rows_rows, preferred_element_type=F32)
        square = term[:, :rows].astype(BF).astype(F32)
        return (coef_second * term[:, rows:] + coef_third * square).astype(BF)

    near = [top, low, plus_t, plus_l, minus_t, minus_l]
    terms = [mixer_rows(v) for v in near]
    far_t, far_l, both, *terms = sync(far_t, far_l, both, *terms)
    far = jnp.concatenate([far_t, far_l], axis=0)
    terms.append(mixer_rows(far))
    targets = jnp.stack(
        [v[i * PAD + capacity, :rows] for v in (*near, far_t, far_l) for i in range(2)], axis=0
    )

    source, position = slot // capacity, slot % capacity
    source_y, source_z = source // 4, source % 4
    away_first = (first - jnp.where(flip, source_z, source_y)) % 4
    away_second = (second - jnp.where(flip, source_y, source_z)) % 4
    away_first, away_second = away_first ^ (away_first >> 1), away_second ^ (away_second >> 1)
    column = (away_second * 4 + away_first) * PAD + position
    compact = (lax.broadcasted_iota(jnp.int32, (1, count * PAD), 1) == column).astype(BF)
    mixer = lax.dot_general(
        jnp.concatenate(terms, axis=0),
        compact,
        (((0,), (1,)), ((), ())),
        preferred_element_type=F32,
    ).astype(BF)

    mixer, targets, by_shard = sync(mixer, targets, by_shard)
    near = by_shard.reshape(8, 2 * rows, width)
    match = (targets.astype(jnp.int32) == ri).astype(jnp.int32)
    slot_of = jnp.where(match == 1, sources[:, None] * capacity + positions(match), -1)

    def placed(i, j):
        place = (slot == slot_of[2 * i : 2 * j].reshape(1, -1)).astype(BF)
        panel = near[i:j].reshape(-1, width)
        return jnp.dot(place, panel, preferred_element_type=F32)

    def product(chunk, panel):
        return lax.dot_general(
            chunk, panel, (((0,), (0,)), ((), ())), preferred_element_type=F32
        )

    update = coef_first * placed(0, 4)
    *got, update = sync(*straight(mixer, send_first), update)
    top, low = jnp.concatenate([mixer, got[0]], axis=0), jnp.concatenate(got[1:], axis=0)
    top, low = sync(top, low)
    plus_t, minus_l = send_second(top, 1), send_second(low, -1)
    update = update + coef_first * placed(4, 8)
    plus_t, minus_l, own_t, own_l, update = sync(plus_t, minus_l, top, low, update)
    plus_l, minus_t = send_second(low, 1), send_second(top, -1)
    far_t, far_l = send_second(plus_t, 1), send_second(minus_l, -1)
    update = update + product(own_t, near[0])
    for chunk, panel in ((own_l, near[1]), (plus_t, near[2]), (minus_l, near[5])):
        (update,) = sync(update)
        update = update + product(chunk, panel)
    plus_l, minus_t, update = sync(plus_l, minus_t, update)
    update = update + product(plus_l, near[3])
    (update,) = sync(update)
    update = update + product(minus_t, near[4])
    far_t, far_l, update = sync(far_t, far_l, update)
    far = jnp.concatenate([far_t, far_l], axis=0)
    update = update + product(far, near[6:].reshape(4 * rows, width))
    return update.astype(BF)


def solution(mesh):
    in_specs = (P("col", "row"), P("col", None))
    out_specs = P("row", "col")
    return jax.shard_map(body, mesh=mesh, in_specs=in_specs, out_specs=out_specs, check_vma=False)
```

```python
import jax
import jax.numpy as jnp
from jax import lax
from jax.experimental import pallas as pl
from jax.experimental.pallas import tpu as pltpu
from jax.sharding import PartitionSpec as P

coef_first = 3.4445
coef_second = -4.775
coef_third = 2.0315

N_X, N_CORE, N_Y, N_Z = 4, 2, 4, 4
PAD = 48
BF = jnp.bfloat16
F32 = jnp.float32


def moved(dx, flip, dy, dz):
    pairs = []
    for x in range(4):
        for k in range(2):
            for y in range(4):
                for z in range(4):
                    to_row = ((x + dx) % 4) * 2 + (k ^ flip)
                    to_col = ((y + dy[k]) % 4) * 4 + (z + dz[k]) % 4
                    pairs.append(((x * 2 + k) * 16 + y * 4 + z, to_row * 16 + to_col))
    return pairs


def send(a, pairs):
    return lax.ppermute(a, ("row", "col"), pairs)


def send_x(a, d):
    return send(a, moved(d, 0, (0, 0), (0, 0)))


def swap_core(a):
    return send(a, moved(0, 1, (0, 0), (0, 0)))


def send_first(a, d):
    return send(a, moved(0, 0, (d, 0), (0, d)))


def send_second(a, d):
    return send(a, moved(0, 0, (0, d), (d, 0)))


def sync(*arrays):
    return lax.optimization_barrier(arrays)


def pick(a, index, axis):
    return lax.dynamic_index_in_dim(a, index % 4, axis=axis, keepdims=False)


def straight(a, move):
    return [move(a, 1), move(a, -1), move(a, 2)]


def total(arrays):
    return sum(v.astype(F32) for v in arrays).astype(BF)


def halves(plus, minus, move):
    half = plus.shape[0] // 2
    return [move(plus[:half], 1), move(minus[half:], -1)]


def regroup_kernel(cols_ref, order_ref, *refs):
    blocks, (near, far) = refs[:8], refs[8:]
    step = pl.program_id(0)

    @pl.when(step < 12)
    def _():
        for i in range(8):
            near[0, order_ref[i]] = blocks[i][0]

    @pl.when(step >= 12)
    def _():
        for i in range(8):
            far[0, order_ref[i]] = blocks[i][0]


def regroup(blocks, cols, order):
    count, rows, width = blocks[0].shape
    spec = pl.BlockSpec((1, rows, width), lambda j, c, o: (c[j], 0, 0))
    near_spec = pl.BlockSpec((1, 8, rows, width), lambda j, c, o: (jnp.minimum(j, 11), 0, 0, 0))
    far_spec = pl.BlockSpec((1, 8, rows, width), lambda j, c, o: (jnp.maximum(j - 12, 0), 0, 0, 0))
    return pl.pallas_call(
        regroup_kernel,
        grid_spec=pltpu.PrefetchScalarGridSpec(
            num_scalar_prefetch=2,
            grid=(count,),
            in_specs=[spec] * 8,
            out_specs=[near_spec, far_spec],
        ),
        out_shape=[
            jax.ShapeDtypeStruct((n, 8, rows, width), blocks[0].dtype) for n in (12, 4)
        ],
        compiler_params=pltpu.CompilerParams(vmem_limit_bytes=32 * 1024 * 1024),
        cost_estimate=pl.CostEstimate(
            flops=0, bytes_accessed=4 * 8 * count * rows * width, transcendentals=0
        ),
    )(cols, order, *blocks)


def body(iterate, route):
    rows, wide = iterate.shape
    groups, count, capacity = 8, 16, 42
    q = rows // groups
    width = wide // 2
    scale = 1.0 / (wide * groups)
    block = count * q
    ri, ci = lax.axis_index("row"), lax.axis_index("col")
    x, core, y, z = ri // 2, ri % 2, ci // 4, ci % 4
    flip = core == 1
    first, second = jnp.where(flip, z, y), jnp.where(flip, y, z)
    rows_rows = (((1,), (1,)), ((), ()))

    by_first = route.reshape(1, rows).astype(BF)
    by_first = jnp.stack([by_first, *straight(by_first, send_first)], axis=1)

    parts = iterate.reshape(groups, q, 2, width).transpose(0, 2, 1, 3)
    parts = lax.all_to_all(parts, "row", 0, 0, tiled=True).reshape(count, q, width)
    parts, by_first = sync(parts, by_first)
    targets = jnp.stack([by_first, *straight(by_first, send_second)], axis=0)
    targets = targets.reshape(count, rows)
    own = lax.all_to_all(parts, "col", 0, 0, tiled=True).reshape(block, width)
    own, route, targets = sync(own, route, targets)

    def gram(panel):
        part = lax.dot_general(panel, own, rows_rows, preferred_element_type=F32)
        return (part * scale).astype(BF).reshape(4, 4, q, block)

    def pick_first(parts, index, axis):
        return jnp.stack(
            [jnp.where(flip, pick(p, index, 1 - axis), pick(p, index, axis)) for p in parts], axis=0
        )

    def messages_first(parts):
        return [pick_first(parts, first + d, 0) for d in (1, -1, 2)]

    def deliver_first(messages):
        return [send_first(m, d) for m, d in zip(messages, (1, -1, 2))]

    def scatter_first(parts):
        return deliver_first(messages_first(parts))

    def gathered(parts, got):
        return total([pick_first(parts, first, 0), *got])

    steps = jnp.asarray([0, 1, 3, 2], jnp.int32)
    order = jnp.stack([((x - d) % 4) * 2 + (core ^ b) for d in (0, 1, 3, 2) for b in range(2)])
    first_of, second_of = (first - steps) % 4, (second - steps) % 4
    sources = jnp.where(
        flip,
        second_of[:, None] * 4 + first_of[None, :],
        first_of[None, :] * 4 + second_of[:, None],
    ).reshape(count)
    slots = capacity * count
    slot = lax.broadcasted_iota(jnp.int32, (slots, 1), 0)

    plus, minus = send_x(own, 1), send_x(own, -1)
    sibling = swap_core(own)
    grams = [gram(own), gram(sibling)]
    got = scatter_first(grams)

    shard = lax.broadcasted_iota(jnp.int32, (count, 1), 0)
    to_shard = (shard == sources[None, :]).astype(BF)
    targets = jnp.dot(to_shard, targets, preferred_element_type=F32).astype(jnp.int32)
    row_of = lax.broadcasted_iota(jnp.int32, (rows, 1), 0)
    upto = (row_of <= lax.broadcasted_iota(jnp.int32, (1, rows), 1)).astype(BF)

    def positions(match):
        counts = jnp.dot(match.astype(BF), upto, preferred_element_type=F32)
        return counts.astype(jnp.int32) - 1

    match = targets == ri
    by_panel = jnp.where(match, shard * capacity + positions(match), -1).reshape(count, groups, q)
    by_panel = jnp.take(by_panel, order, axis=1).swapaxes(0, 1).reshape(groups, block)
    labels = lax.broadcasted_iota(jnp.int32, (groups, 1), 0)
    match = route.reshape(1, rows) == labels
    row_slot = jnp.sum(jnp.where(match, labels * PAD + positions(match), 0), axis=0)
    row_slot = jnp.take(row_slot.reshape(groups, q), order, axis=0).reshape(1, rows)
    choose = (lax.broadcasted_iota(jnp.int32, (groups * PAD, 1), 0) == row_slot).astype(BF)

    def placed(i, panel):
        place = (slot == by_panel[i].reshape(1, block)).astype(BF)
        return jnp.dot(place, panel, preferred_element_type=F32)

    *got, plus, minus, by_panel, choose = sync(*got, plus, minus, by_panel, choose)
    sum_0 = gathered(grams, got)

    plus_s, minus_s = sync(swap_core(plus), swap_core(minus))
    far = halves(plus, minus, send_x)
    grams = [gram(plus), gram(plus_s), gram(minus), gram(minus_s)]
    *messages, own_x, sibling_x = sync(*messages_first(grams), own, sibling)
    got = deliver_first(messages)
    update = placed(0, own_x)
    (update,) = sync(update)
    update = update + placed(1, sibling_x)
    *got, far_a, far_b, update = sync(*got, *far, update)
    sum_1 = gathered(grams, got)

    far = jnp.concatenate([far_a, far_b], axis=0)
    far_s = swap_core(far)
    grams = [gram(far), gram(far_s)]
    *messages, plus_x, sibling_x = sync(*messages_first(grams), plus, plus_s)
    got = deliver_first(messages)
    update = update + placed(2, plus_x)
    (update,) = sync(update)
    update = update + placed(3, sibling_x)
    *got, update = sync(*got, update)
    sum_2 = gathered(grams, got)

    sums = jnp.concatenate([sum_0, sum_1, sum_2], axis=0)
    messages = [pick(sums, second + d, 1) for d in (1, -1, 2)]
    *messages, minus_x, sibling_x = sync(*messages, minus, minus_s)
    got = [send_second(m, d) for m, d in zip(messages, (1, -1, 2))]
    update = update + placed(4, minus_x)
    (update,) = sync(update)
    update = update + placed(5, sibling_x)
    *got, update = sync(*got, update)
    share = total([pick(sums, second, 1), *got])

    routed = jnp.dot(choose, share.reshape(rows, block), preferred_element_type=F32).astype(BF)
    routed = routed.reshape(4, 2, PAD, block)
    other = swap_core(jnp.where(flip, routed[:, 0], routed[:, 1]))
    routed = jnp.stack([jnp.where(flip, routed[:, 1], routed[:, 0]), other], axis=1)
    *got, share = sync(*[send_x(pick(routed, x + d, 0), d) for d in (1, -1, 2)], share)
    lanes = [v[b] for v in (pick(routed, x, 0), *got) for b in range(2)]
    lanes = jnp.concatenate(lanes, axis=1)

    lanes, share, far_x, sibling_x = sync(lanes, share, far, far_s)
    got = straight(lanes, send_first)
    update = update + placed(6, far_x)
    ordered = []
    for t in range(4):
        d = (x - t) % 4
        d = d ^ (d >> 1)
        for k in range(2):
            ordered.append(lax.dynamic_index_in_dim(share, d * 2 + (core ^ k), 0, keepdims=False))
    gram_share = jnp.concatenate(ordered, axis=0)
    *got, gram_share, update = sync(*got, gram_share, update)

    top, low = jnp.concatenate([lanes, got[0]], axis=0), jnp.concatenate(got[1:], axis=0)
    top, low, gram_share, update = sync(top, low, gram_share, update)
    plus_t, minus_l = send_second(top, 1), send_second(low, -1)
    gram_p, gram_m = send_x(gram_share, 1), send_x(gram_share, -1)
    gram_s = swap_core(gram_share)
    update = update + placed(7, sibling_x)
    plus_t, minus_l, gram_p, gram_m, gram_s, update = sync(
        plus_t, minus_l, gram_p, gram_m, gram_s, update
    )
    gram_f = send_x(gram_share, 2)
    plus_l, minus_t = send_second(low, 1), send_second(top, -1)
    far_t, far_l = send_second(plus_t, 1), send_second(minus_l, -1)
    gram_ps, gram_ms, gram_fs = swap_core(gram_p), swap_core(gram_m), swap_core(gram_f)
    gram_rows = jnp.concatenate(
        [gram_share, gram_s, gram_p, gram_ps, gram_m, gram_ms, gram_f, gram_fs], axis=1
    )
    place = (slot == by_panel.reshape(1, groups * block)).astype(BF)
    gram_cols = lax.dot_general(gram_rows, place, rows_rows, preferred_element_type=F32)
    gram_cols = gram_cols.astype(BF)

    def square_rows(chunk):
        term = lax.dot_general(chunk, gram_rows, rows_rows, preferred_element_type=F32)
        return term.astype(BF)

    terms = [square_rows(v) for v in (top, low, plus_t, plus_l, minus_t, minus_l)]
    far_t, far_l, gram_cols, gram_rows, *terms = sync(far_t, far_l, gram_cols, gram_rows, *terms)
    terms.append(square_rows(jnp.concatenate([far_t, far_l], axis=0)))

    source, position = slot // capacity, slot % capacity
    source_y, source_z = source // 4, source % 4
    away_first = (first - jnp.where(flip, source_z, source_y)) % 4
    away_second = (second - jnp.where(flip, source_y, source_z)) % 4
    away_first, away_second = away_first ^ (away_first >> 1), away_second ^ (away_second >> 1)
    column = (away_second * 4 + away_first) * PAD + position
    compact = (lax.broadcasted_iota(jnp.int32, (1, count * PAD), 1) == column).astype(BF)
    square = lax.dot_general(
        jnp.concatenate(terms, axis=0),
        compact,
        (((0,), (1,)), ((), ())),
        preferred_element_type=F32,
    )
    square = square.astype(BF).astype(F32)
    mixer = (coef_second * gram_cols.astype(F32) + coef_third * square).astype(BF)

    panels = [own, sibling, plus, plus_s, minus, minus_s, far, far_s]
    mixer, *panels = sync(mixer, *panels)
    near, away = regroup([v.reshape(count, q, width) for v in panels], sources, order)

    def product(chunk, panel):
        return lax.dot_general(
            chunk, panel, (((0,), (0,)), ((), ())), preferred_element_type=F32
        )

    *got, near, away = sync(*straight(mixer, send_first), near, away)
    near = near.reshape(6, 2 * rows, width)
    top, low = jnp.concatenate([mixer, got[0]], axis=0), jnp.concatenate(got[1:], axis=0)
    top, low = sync(top, low)
    plus_t, minus_l = send_second(top, 1), send_second(low, -1)
    plus_t, minus_l, own_t, own_l = sync(plus_t, minus_l, top, low)
    plus_l, minus_t = send_second(low, 1), send_second(top, -1)
    far_t, far_l = send_second(plus_t, 1), send_second(minus_l, -1)
    update = coef_first * update + product(own_t, near[0])
    for chunk, panel in ((own_l, near[1]), (plus_t, near[2]), (minus_l, near[5])):
        (update,) = sync(update)
        update = update + product(chunk, panel)
    plus_l, minus_t, update = sync(plus_l, minus_t, update)
    update = update + product(plus_l, near[3])
    (update,) = sync(update)
    update = update + product(minus_t, near[4])
    far_t, far_l, update = sync(far_t, far_l, update)
    update = update + product(jnp.concatenate([far_t, far_l], axis=0), away.reshape(4 * rows, width))
    return update.astype(BF)


def solution(mesh):
    in_specs = (P("col", "row"), P("col", None))
    out_specs = P("row", "col")
    return jax.shard_map(body, mesh=mesh, in_specs=in_specs, out_specs=out_specs, check_vma=False)
```

```python
import jax
import jax.numpy as jnp
from jax import lax
from jax.experimental import pallas as pl
from jax.experimental.pallas import tpu as pltpu
from jax.sharding import PartitionSpec as P

coef_first = 3.4445
coef_second = -4.775
coef_third = 2.0315

N_X, N_CORE, N_Y, N_Z = 4, 2, 4, 4
PAD = 48
BF = jnp.bfloat16
F32 = jnp.float32


def moved(dx, flip, dy, dz):
    pairs = []
    for x in range(4):
        for k in range(2):
            for y in range(4):
                for z in range(4):
                    to_row = ((x + dx) % 4) * 2 + (k ^ flip)
                    to_col = ((y + dy[k]) % 4) * 4 + (z + dz[k]) % 4
                    pairs.append(((x * 2 + k) * 16 + y * 4 + z, to_row * 16 + to_col))
    return pairs


def send(a, pairs):
    return lax.ppermute(a, ("row", "col"), pairs)


def send_x(a, d):
    return send(a, moved(d, 0, (0, 0), (0, 0)))


def swap_core(a):
    return send(a, moved(0, 1, (0, 0), (0, 0)))


def send_first(a, d):
    return send(a, moved(0, 0, (d, 0), (0, d)))


def send_second(a, d):
    return send(a, moved(0, 0, (0, d), (d, 0)))


def sync(*arrays):
    return lax.optimization_barrier(arrays)


def pick(a, index, axis):
    return lax.dynamic_index_in_dim(a, index % 4, axis=axis, keepdims=False)


def straight(a, move):
    return [move(a, 1), move(a, -1), move(a, 2)]


def total(arrays):
    return sum(v.astype(F32) for v in arrays).astype(BF)


def halves(plus, minus, move):
    half = plus.shape[0] // 2
    return [move(plus[:half], 1), move(minus[half:], -1)]


def regroup_kernel(cols_ref, order_ref, *refs):
    blocks, (near, far) = refs[:8], refs[8:]
    step = pl.program_id(0)

    @pl.when(step < 12)
    def _():
        for i in range(8):
            near[0, order_ref[i]] = blocks[i][0]

    @pl.when(step >= 12)
    def _():
        for i in range(8):
            far[0, order_ref[i]] = blocks[i][0]


def regroup(blocks, cols, order):
    count, rows, width = blocks[0].shape
    spec = pl.BlockSpec((1, rows, width), lambda j, c, o: (c[j], 0, 0))
    near_spec = pl.BlockSpec((1, 8, rows, width), lambda j, c, o: (jnp.minimum(j, 11), 0, 0, 0))
    far_spec = pl.BlockSpec((1, 8, rows, width), lambda j, c, o: (jnp.maximum(j - 12, 0), 0, 0, 0))
    return pl.pallas_call(
        regroup_kernel,
        grid_spec=pltpu.PrefetchScalarGridSpec(
            num_scalar_prefetch=2,
            grid=(count,),
            in_specs=[spec] * 8,
            out_specs=[near_spec, far_spec],
        ),
        out_shape=[
            jax.ShapeDtypeStruct((n, 8, rows, width), blocks[0].dtype) for n in (12, 4)
        ],
        compiler_params=pltpu.CompilerParams(vmem_limit_bytes=32 * 1024 * 1024),
        cost_estimate=pl.CostEstimate(
            flops=0, bytes_accessed=4 * 8 * count * rows * width, transcendentals=0
        ),
    )(cols, order, *blocks)


def body(iterate, route):
    rows, wide = iterate.shape
    groups, count, capacity = 8, 16, 42
    q = rows // groups
    width = wide // 2
    scale = 1.0 / (wide * groups)
    block = count * q
    ri, ci = lax.axis_index("row"), lax.axis_index("col")
    x, core, y, z = ri // 2, ri % 2, ci // 4, ci % 4
    flip = core == 1
    first, second = jnp.where(flip, z, y), jnp.where(flip, y, z)
    rows_rows = (((1,), (1,)), ((), ()))

    by_first = route.reshape(1, rows).astype(BF)
    by_first = jnp.stack([by_first, *straight(by_first, send_first)], axis=1)

    parts = iterate.reshape(groups, q, 2, width).transpose(0, 2, 1, 3)
    parts = lax.all_to_all(parts, "row", 0, 0, tiled=True).reshape(count, q, width)
    parts, by_first = sync(parts, by_first)
    targets = jnp.stack([by_first, *straight(by_first, send_second)], axis=0)
    targets = targets.reshape(count, rows)
    own = lax.all_to_all(parts, "col", 0, 0, tiled=True).reshape(block, width)
    own, route, targets = sync(own, route, targets)

    def gram(panel):
        part = lax.dot_general(panel, own, rows_rows, preferred_element_type=F32)
        return (part * scale).astype(BF).reshape(4, 4, q, block)

    def pick_first(parts, index, axis):
        return jnp.stack(
            [jnp.where(flip, pick(p, index, 1 - axis), pick(p, index, axis)) for p in parts], axis=0
        )

    def messages_first(parts):
        return [pick_first(parts, first + d, 0) for d in (1, -1, 2)]

    def deliver_first(messages):
        return [send_first(m, d) for m, d in zip(messages, (1, -1, 2))]

    def scatter_first(parts):
        return deliver_first(messages_first(parts))

    def gathered(parts, got):
        return total([pick_first(parts, first, 0), *got])

    steps = jnp.asarray([0, 1, 3, 2], jnp.int32)
    order = jnp.stack([((x - d) % 4) * 2 + (core ^ b) for d in (0, 1, 3, 2) for b in range(2)])
    first_of, second_of = (first - steps) % 4, (second - steps) % 4
    sources = jnp.where(
        flip,
        second_of[:, None] * 4 + first_of[None, :],
        first_of[None, :] * 4 + second_of[:, None],
    ).reshape(count)
    slots = capacity * count
    slot = lax.broadcasted_iota(jnp.int32, (slots, 1), 0)

    plus, minus = send_x(own, 1), send_x(own, -1)
    sibling = swap_core(own)
    grams = [gram(own), gram(sibling)]
    got = scatter_first(grams)

    shard = lax.broadcasted_iota(jnp.int32, (count, 1), 0)
    to_shard = (shard == sources[None, :]).astype(BF)
    targets = jnp.dot(to_shard, targets, preferred_element_type=F32).astype(jnp.int32)
    row_of = lax.broadcasted_iota(jnp.int32, (rows, 1), 0)
    upto = (row_of <= lax.broadcasted_iota(jnp.int32, (1, rows), 1)).astype(BF)

    def positions(match):
        counts = jnp.dot(match.astype(BF), upto, preferred_element_type=F32)
        return counts.astype(jnp.int32) - 1

    match = targets == ri
    by_panel = jnp.where(match, shard * capacity + positions(match), -1).reshape(count, groups, q)
    by_panel = jnp.take(by_panel, order, axis=1).swapaxes(0, 1).reshape(groups, block)
    labels = lax.broadcasted_iota(jnp.int32, (groups, 1), 0)
    match = route.reshape(1, rows) == labels
    row_slot = jnp.sum(jnp.where(match, labels * PAD + positions(match), 0), axis=0)
    row_slot = row_slot.reshape(1, rows)
    choose = (lax.broadcasted_iota(jnp.int32, (groups * PAD, 1), 0) == row_slot).astype(BF)

    def placed(i, panel):
        place = (slot == by_panel[i].reshape(1, block)).astype(BF)
        return jnp.dot(place, panel, preferred_element_type=F32)

    *got, plus, minus, by_panel, choose = sync(*got, plus, minus, by_panel, choose)
    sum_0 = gathered(grams, got)

    def put(sums, parts, d):
        for b in range(2):
            s = ((x - d) % 4) * 2 + (core ^ b)
            sums = lax.dynamic_update_index_in_dim(sums, parts[b], s, 0)
        return sums

    plus_s, minus_s = sync(swap_core(plus), swap_core(minus))
    far = halves(plus, minus, send_x)
    grams = [gram(plus), gram(plus_s), gram(minus), gram(minus_s)]
    *messages, own_x, sibling_x = sync(*messages_first(grams), own, sibling)
    got = deliver_first(messages)
    mine = pick_first(grams, first, 0)
    update = placed(0, own_x)
    (update,) = sync(update)
    update = update + placed(1, sibling_x)
    sums = put(jnp.zeros((groups, 4, q, block), BF), sum_0, 0)
    *got_1, far_a, far_b, update, sums, mine = sync(*got, *far, update, sums, mine)

    far = jnp.concatenate([far_a, far_b], axis=0)
    far_s = swap_core(far)
    grams = [gram(far), gram(far_s)]
    messages = messages_first(grams)
    *messages, plus_x, sibling_x, mine, g0, g1, g2 = sync(*messages, plus, plus_s, mine, *got_1)
    got = deliver_first(messages)
    sum_1 = total([mine, g0, g1, g2])
    sums = put(put(sums, sum_1[:2], 1), sum_1[2:], 3)
    update = update + placed(2, plus_x)
    (update,) = sync(update)
    update = update + placed(3, sibling_x)
    *got, update, sums = sync(*got, update, sums)
    sums = put(sums, gathered(grams, got), 2)

    messages = [pick(sums, second + d, 1) for d in (1, -1, 2)]
    *messages, minus_x, sibling_x = sync(*messages, minus, minus_s)
    got = [send_second(m, d) for m, d in zip(messages, (1, -1, 2))]
    update = update + placed(4, minus_x)
    (update,) = sync(update)
    update = update + placed(5, sibling_x)
    *got, update = sync(*got, update)
    share = total([pick(sums, second, 1), *got])
    gram_share = share.reshape(rows, block)

    routed = jnp.dot(choose, gram_share, preferred_element_type=F32).astype(BF)
    routed = routed.reshape(4, 2, PAD, block)
    other = swap_core(jnp.where(flip, routed[:, 0], routed[:, 1]))
    routed = jnp.stack([jnp.where(flip, routed[:, 1], routed[:, 0]), other], axis=1)
    *got, gram_share = sync(*[send_x(pick(routed, x + d, 0), d) for d in (1, -1, 2)], gram_share)
    lanes = [v[b] for v in (pick(routed, x, 0), *got) for b in range(2)]
    lanes = jnp.concatenate(lanes, axis=1)

    lanes, gram_share = sync(lanes, gram_share)
    got = straight(lanes, send_first)
    gram_p, gram_m = send_x(gram_share, 1), send_x(gram_share, -1)
    *got, gram_p, gram_m, gram_ps, gram_ms = sync(
        *got, gram_p, gram_m, swap_core(gram_p), swap_core(gram_m)
    )

    top, low = jnp.concatenate([lanes, got[0]], axis=0), jnp.concatenate(got[1:], axis=0)
    top, low, gram_share = sync(top, low, gram_share)
    plus_t, minus_l = send_second(top, 1), send_second(low, -1)
    gram_f = send_x(gram_share, 2)
    gram_s, top_x, low_x = sync(swap_core(gram_share), top, low)
    plus_l, minus_t = send_second(low_x, 1), send_second(top_x, -1)
    far_t, far_l = send_second(plus_t, 1), send_second(minus_l, -1)
    gram_fs = swap_core(gram_f)
    gram_rows = jnp.concatenate(
        [gram_share, gram_s, gram_p, gram_ps, gram_m, gram_ms, gram_f, gram_fs], axis=1
    )
    place = (slot == by_panel.reshape(1, groups * block)).astype(BF)
    gram_cols = lax.dot_general(gram_rows, place, rows_rows, preferred_element_type=F32)
    gram_cols = gram_cols.astype(BF)

    def square_rows(chunk):
        term = lax.dot_general(chunk, gram_rows, rows_rows, preferred_element_type=F32)
        return term.astype(BF)

    terms = [square_rows(v) for v in (top, low, plus_t, plus_l, minus_t, minus_l)]
    far_t, far_l, gram_cols, gram_rows, *terms = sync(far_t, far_l, gram_cols, gram_rows, *terms)
    terms.append(square_rows(jnp.concatenate([far_t, far_l], axis=0)))

    source, position = slot // capacity, slot % capacity
    source_y, source_z = source // 4, source % 4
    away_first = (first - jnp.where(flip, source_z, source_y)) % 4
    away_second = (second - jnp.where(flip, source_y, source_z)) % 4
    away_first, away_second = away_first ^ (away_first >> 1), away_second ^ (away_second >> 1)
    column = (away_second * 4 + away_first) * PAD + position
    compact = (lax.broadcasted_iota(jnp.int32, (1, count * PAD), 1) == column).astype(BF)
    square = lax.dot_general(
        jnp.concatenate(terms, axis=0),
        compact,
        (((0,), (1,)), ((), ())),
        preferred_element_type=F32,
    )
    square = square.astype(BF).astype(F32)
    mixer = (coef_second * gram_cols.astype(F32) + coef_third * square).astype(BF)

    panels = [own, sibling, plus, plus_s, minus, minus_s, far, far_s]
    mixer, *panels = sync(mixer, *panels)
    near, away = regroup([v.reshape(count, q, width) for v in panels], sources, order)

    def product(chunk, panel):
        return lax.dot_general(
            chunk, panel, (((0,), (0,)), ((), ())), preferred_element_type=F32
        )

    *got, near, away = sync(*straight(mixer, send_first), near, away)
    near = near.reshape(6, 2 * rows, width)
    top, low = jnp.concatenate([mixer, got[0]], axis=0), jnp.concatenate(got[1:], axis=0)
    top, low, far_x, sibling_x = sync(top, low, far, far_s)
    plus_t, minus_l = send_second(top, 1), send_second(low, -1)
    update, own_t, own_l = sync(update + placed(6, far_x), top, low)
    plus_l, minus_t = send_second(own_l, 1), send_second(own_t, -1)
    update = update + placed(7, sibling_x)
    plus_t, minus_l, update = sync(plus_t, minus_l, update)
    far_t, far_l = send_second(plus_t, 1), send_second(minus_l, -1)
    update = coef_first * update + product(own_t, near[0])
    for chunk, panel in ((own_l, near[1]), (plus_t, near[2]), (minus_l, near[5])):
        (update,) = sync(update)
        update = update + product(chunk, panel)
    plus_l, minus_t, update = sync(plus_l, minus_t, update)
    update = update + product(plus_l, near[3])
    (update,) = sync(update)
    update = update + product(minus_t, near[4])
    far_t, far_l, update = sync(far_t, far_l, update)
    update = update + product(jnp.concatenate([far_t, far_l], axis=0), away.reshape(4 * rows, width))
    return update.astype(BF)


def solution(mesh):
    in_specs = (P("col", "row"), P("col", None))
    out_specs = P("row", "col")
    return jax.shard_map(body, mesh=mesh, in_specs=in_specs, out_specs=out_specs, check_vma=False)
```

```python
import jax
import jax.numpy as jnp
from jax import lax
from jax.experimental import pallas as pl
from jax.experimental.pallas import tpu as pltpu
from jax.sharding import PartitionSpec as P

coef_first = 3.4445
coef_second = -4.775
coef_third = 2.0315

N_X, N_CORE, N_Y, N_Z = 4, 2, 4, 4
PAD = 48
BF = jnp.bfloat16
F32 = jnp.float32


def moved(dx, flip, dy, dz):
    pairs = []
    for x in range(4):
        for k in range(2):
            for y in range(4):
                for z in range(4):
                    to_row = ((x + dx) % 4) * 2 + (k ^ flip)
                    to_col = ((y + dy[k]) % 4) * 4 + (z + dz[k]) % 4
                    pairs.append(((x * 2 + k) * 16 + y * 4 + z, to_row * 16 + to_col))
    return pairs


def send(a, pairs):
    return lax.ppermute(a, ("row", "col"), pairs)


def send_x(a, d):
    return send(a, moved(d, 0, (0, 0), (0, 0)))


def swap_core(a):
    return send(a, moved(0, 1, (0, 0), (0, 0)))


def send_first(a, d):
    return send(a, moved(0, 0, (d, 0), (0, d)))


def send_second(a, d):
    return send(a, moved(0, 0, (0, d), (d, 0)))


def sync(*arrays):
    return lax.optimization_barrier(arrays)


def pick(a, index, axis):
    return lax.dynamic_index_in_dim(a, index % 4, axis=axis, keepdims=False)


def straight(a, move):
    return [move(a, 1), move(a, -1), move(a, 2)]


def total(arrays):
    return sum(v.astype(F32) for v in arrays).astype(BF)


def halves(plus, minus, move):
    half = plus.shape[0] // 2
    return [move(plus[:half], 1), move(minus[half:], -1)]


def regroup_kernel(cols_ref, order_ref, *refs):
    blocks, (near, far) = refs[:8], refs[8:]
    step = pl.program_id(0)

    @pl.when(step < 12)
    def _():
        for i in range(8):
            near[0, order_ref[i]] = blocks[i][0]

    @pl.when(step >= 12)
    def _():
        for i in range(8):
            far[0, order_ref[i]] = blocks[i][0]


def regroup(blocks, cols, order):
    count, rows, width = blocks[0].shape
    spec = pl.BlockSpec((1, rows, width), lambda j, c, o: (c[j], 0, 0))
    near_spec = pl.BlockSpec((1, 8, rows, width), lambda j, c, o: (jnp.minimum(j, 11), 0, 0, 0))
    far_spec = pl.BlockSpec((1, 8, rows, width), lambda j, c, o: (jnp.maximum(j - 12, 0), 0, 0, 0))
    return pl.pallas_call(
        regroup_kernel,
        grid_spec=pltpu.PrefetchScalarGridSpec(
            num_scalar_prefetch=2,
            grid=(count,),
            in_specs=[spec] * 8,
            out_specs=[near_spec, far_spec],
        ),
        out_shape=[
            jax.ShapeDtypeStruct((n, 8, rows, width), blocks[0].dtype) for n in (12, 4)
        ],
        compiler_params=pltpu.CompilerParams(vmem_limit_bytes=32 * 1024 * 1024),
        cost_estimate=pl.CostEstimate(
            flops=0, bytes_accessed=4 * 8 * count * rows * width, transcendentals=0
        ),
    )(cols, order, *blocks)


def body(iterate, route):
    rows, wide = iterate.shape
    groups, count, capacity = 8, 16, 42
    q = rows // groups
    width = wide // 2
    scale = 1.0 / (wide * groups)
    block = count * q
    ri, ci = lax.axis_index("row"), lax.axis_index("col")
    x, core, y, z = ri // 2, ri % 2, ci // 4, ci % 4
    flip = core == 1
    first, second = jnp.where(flip, z, y), jnp.where(flip, y, z)
    rows_rows = (((1,), (1,)), ((), ()))

    by_first = route.reshape(1, rows).astype(BF)
    by_first = jnp.stack([by_first, *straight(by_first, send_first)], axis=1)

    parts = iterate.reshape(groups, q, 2, width).transpose(0, 2, 1, 3)
    parts = lax.all_to_all(parts, "row", 0, 0, tiled=True).reshape(count, q, width)
    parts, by_first = sync(parts, by_first)
    targets = jnp.stack([by_first, *straight(by_first, send_second)], axis=0)
    targets = targets.reshape(count, rows)
    own = lax.all_to_all(parts, "col", 0, 0, tiled=True).reshape(block, width)
    own, route, targets = sync(own, route, targets)

    def gram(panel):
        part = lax.dot_general(panel, own, rows_rows, preferred_element_type=F32)
        return (part * scale).astype(BF).reshape(4, 4, q, block)

    def pick_first(parts, index, axis):
        return jnp.stack(
            [jnp.where(flip, pick(p, index, 1 - axis), pick(p, index, axis)) for p in parts], axis=0
        )

    def messages_first(parts):
        return [pick_first(parts, first + d, 0) for d in (1, -1, 2)]

    def deliver_first(messages):
        return [send_first(m, d) for m, d in zip(messages, (1, -1, 2))]

    def scatter_first(parts):
        return deliver_first(messages_first(parts))

    def gathered(parts, got):
        return total([pick_first(parts, first, 0), *got])

    steps = jnp.asarray([0, 1, 3, 2], jnp.int32)
    order = jnp.stack([((x - d) % 4) * 2 + (core ^ b) for d in (0, 1, 3, 2) for b in range(2)])
    first_of, second_of = (first - steps) % 4, (second - steps) % 4
    sources = jnp.where(
        flip,
        second_of[:, None] * 4 + first_of[None, :],
        first_of[None, :] * 4 + second_of[:, None],
    ).reshape(count)
    slots = capacity * count
    slot = lax.broadcasted_iota(jnp.int32, (slots, 1), 0)

    plus, minus = send_x(own, 1), send_x(own, -1)
    sibling = swap_core(own)
    grams = [gram(own), gram(sibling)]
    got = scatter_first(grams)

    shard = lax.broadcasted_iota(jnp.int32, (count, 1), 0)
    to_shard = (shard == sources[None, :]).astype(BF)
    targets = jnp.dot(to_shard, targets, preferred_element_type=F32).astype(jnp.int32)
    row_of = lax.broadcasted_iota(jnp.int32, (rows, 1), 0)
    upto = (row_of <= lax.broadcasted_iota(jnp.int32, (1, rows), 1)).astype(BF)

    def positions(match):
        counts = jnp.dot(match.astype(BF), upto, preferred_element_type=F32)
        return counts.astype(jnp.int32) - 1

    match = targets == ri
    by_panel = jnp.where(match, shard * capacity + positions(match), -1).reshape(count, groups, q)
    by_panel = jnp.take(by_panel, order, axis=1).swapaxes(0, 1).reshape(groups, block)
    labels = lax.broadcasted_iota(jnp.int32, (groups, 1), 0)
    match = route.reshape(1, rows) == labels
    row_slot = jnp.sum(jnp.where(match, labels * PAD + positions(match), 0), axis=0)
    row_slot = row_slot.reshape(1, rows)
    choose = (lax.broadcasted_iota(jnp.int32, (groups * PAD, 1), 0) == row_slot).astype(BF)

    def placed(i, panel):
        place = (slot == by_panel[i].reshape(1, block)).astype(BF)
        return jnp.dot(place, panel, preferred_element_type=F32)

    mine = pick_first(grams, first, 0)
    *got_0, plus, minus, by_panel, choose, mine_0 = sync(
        *got, plus, minus, by_panel, choose, mine
    )

    def put(sums, parts, d):
        for b in range(2):
            s = ((x - d) % 4) * 2 + (core ^ b)
            sums = lax.dynamic_update_index_in_dim(sums, parts[b], s, 0)
        return sums

    plus_s, minus_s = sync(swap_core(plus), swap_core(minus))
    far = halves(plus, minus, send_x)
    grams = [gram(plus), gram(plus_s), gram(minus), gram(minus_s)]
    *messages, own_x, sibling_x, g0, g1, g2, mine_0 = sync(
        *messages_first(grams), own, sibling, *got_0, mine_0
    )
    got = deliver_first(messages)
    mine = pick_first(grams, first, 0)
    update = placed(0, own_x)
    (update,) = sync(update)
    update = update + placed(1, sibling_x)
    sums = put(jnp.zeros((groups, 4, q, block), BF), total([mine_0, g0, g1, g2]), 0)
    *got_1, far_a, far_b, update, sums, mine = sync(*got, *far, update, sums, mine)

    far = jnp.concatenate([far_a, far_b], axis=0)
    far_s = swap_core(far)
    grams = [gram(far), gram(far_s)]
    messages = messages_first(grams)
    *messages, plus_x, sibling_x, mine, g0, g1, g2 = sync(*messages, plus, plus_s, mine, *got_1)
    got = deliver_first(messages)
    sum_1 = total([mine, g0, g1, g2])
    sums = put(put(sums, sum_1[:2], 1), sum_1[2:], 3)
    update = update + placed(2, plus_x)
    (update,) = sync(update)
    update = update + placed(3, sibling_x)
    *got, update, sums = sync(*got, update, sums)
    sums = put(sums, gathered(grams, got), 2)

    messages = [pick(sums, second + d, 1) for d in (1, -1, 2)]
    *messages, minus_x, sibling_x = sync(*messages, minus, minus_s)
    got = [send_second(m, d) for m, d in zip(messages, (1, -1, 2))]
    update = update + placed(4, minus_x)
    (update,) = sync(update)
    update = update + placed(5, sibling_x)
    *got, update = sync(*got, update)
    share = total([pick(sums, second, 1), *got])
    gram_share = share.reshape(rows, block)

    routed = jnp.dot(choose, gram_share, preferred_element_type=F32).astype(BF)
    routed = routed.reshape(4, 2, PAD, block)
    other = swap_core(jnp.where(flip, routed[:, 0], routed[:, 1]))
    routed = jnp.stack([jnp.where(flip, routed[:, 1], routed[:, 0]), other], axis=1)
    *got, gram_share = sync(*[send_x(pick(routed, x + d, 0), d) for d in (1, -1, 2)], gram_share)
    lanes = [v[b] for v in (pick(routed, x, 0), *got) for b in range(2)]
    lanes = jnp.concatenate(lanes, axis=1)

    lanes, gram_share, far_x, sibling_x = sync(lanes, gram_share, far, far_s)
    got = straight(lanes, send_first)
    update = update + placed(6, far_x)
    gram_p, gram_m = send_x(gram_share, 1), send_x(gram_share, -1)
    *got, gram_p, gram_m, gram_ps, gram_ms, update = sync(
        *got, gram_p, gram_m, swap_core(gram_p), swap_core(gram_m), update
    )

    top, low = jnp.concatenate([lanes, got[0]], axis=0), jnp.concatenate(got[1:], axis=0)
    top, low, gram_share = sync(top, low, gram_share)
    plus_t, minus_l = send_second(top, 1), send_second(low, -1)
    gram_f = send_x(gram_share, 2)
    gram_s, top_x, low_x = sync(swap_core(gram_share), top, low)
    plus_l, minus_t = send_second(low_x, 1), send_second(top_x, -1)
    far_t, far_l = send_second(plus_t, 1), send_second(minus_l, -1)
    gram_fs = swap_core(gram_f)
    gram_rows = jnp.concatenate(
        [gram_share, gram_s, gram_p, gram_ps, gram_m, gram_ms, gram_f, gram_fs], axis=1
    )
    place = (slot == by_panel.reshape(1, groups * block)).astype(BF)
    gram_cols = lax.dot_general(place, gram_rows, rows_rows, preferred_element_type=F32)
    gram_cols = gram_cols.astype(BF)

    def square_rows(chunk):
        term = lax.dot_general(chunk, gram_rows, rows_rows, preferred_element_type=F32)
        return term.astype(BF)

    terms = [square_rows(v) for v in (top, low, plus_t, plus_l, minus_t, minus_l)]
    update = coef_first * (update + placed(7, sibling_x))
    far_t, far_l, gram_cols, gram_rows, update, *terms = sync(
        far_t, far_l, gram_cols, gram_rows, update, *terms
    )
    terms.append(square_rows(jnp.concatenate([far_t, far_l], axis=0)))

    source, position = slot // capacity, slot % capacity
    source_y, source_z = source // 4, source % 4
    away_first = (first - jnp.where(flip, source_z, source_y)) % 4
    away_second = (second - jnp.where(flip, source_y, source_z)) % 4
    away_first, away_second = away_first ^ (away_first >> 1), away_second ^ (away_second >> 1)
    column = (away_second * 4 + away_first) * PAD + position
    compact = (lax.broadcasted_iota(jnp.int32, (1, count * PAD), 1) == column).astype(BF)
    square = jnp.dot(compact, jnp.concatenate(terms, axis=0), preferred_element_type=F32)
    square = square.astype(BF).astype(F32)
    mixer = (coef_second * gram_cols.astype(F32) + coef_third * square).astype(BF)

    panels = [own, sibling, plus, plus_s, minus, minus_s, far, far_s]
    mixer, *panels = sync(mixer, *panels)
    near, away = regroup([v.reshape(count, q, width) for v in panels], sources, order)

    def product(chunk, panel):
        return jnp.dot(chunk, panel, preferred_element_type=F32)

    *got, near, away = sync(*straight(mixer, send_first), near, away)
    near = near.reshape(6, 2 * rows, width)
    top, low = jnp.concatenate([mixer, got[0]], axis=1), jnp.concatenate(got[1:], axis=1)
    top, low = sync(top, low)
    plus_t, minus_l = send_second(top, 1), send_second(low, -1)
    update, top, low = sync(update + product(top, near[0]), top, low)
    plus_l, minus_t = send_second(low, 1), send_second(top, -1)
    update = update + product(low, near[1])
    plus_t, minus_l, update = sync(plus_t, minus_l, update)
    far_t, far_l = send_second(plus_t, 1), send_second(minus_l, -1)
    for chunk, panel in ((plus_t, near[2]), (minus_l, near[5])):
        (update,) = sync(update)
        update = update + product(chunk, panel)
    plus_l, minus_t, update = sync(plus_l, minus_t, update)
    update = update + product(plus_l, near[3])
    (update,) = sync(update)
    update = update + product(minus_t, near[4])
    far_t, far_l, update = sync(far_t, far_l, update)
    far = jnp.concatenate([far_t, far_l], axis=1)
    update = update + product(far, away.reshape(4 * rows, width))
    return update.astype(BF)


def solution(mesh):
    in_specs = (P("col", "row"), P("col", None))
    out_specs = P("row", "col")
    return jax.shard_map(body, mesh=mesh, in_specs=in_specs, out_specs=out_specs, check_vma=False)
```

```python
import jax
import jax.numpy as jnp
from jax import lax
from jax.experimental import pallas as pl
from jax.experimental.pallas import tpu as pltpu
from jax.sharding import PartitionSpec as P

coef_first = 3.4445
coef_second = -4.775
coef_third = 2.0315

N_X, N_CORE, N_Y, N_Z = 4, 2, 4, 4
PAD = 48
BF = jnp.bfloat16
F32 = jnp.float32


def moved(dx, flip, dy, dz):
    pairs = []
    for x in range(4):
        for k in range(2):
            for y in range(4):
                for z in range(4):
                    to_row = ((x + dx) % 4) * 2 + (k ^ flip)
                    to_col = ((y + dy[k]) % 4) * 4 + (z + dz[k]) % 4
                    pairs.append(((x * 2 + k) * 16 + y * 4 + z, to_row * 16 + to_col))
    return pairs


def send(a, pairs):
    return lax.ppermute(a, ("row", "col"), pairs)


def send_x(a, d):
    return send(a, moved(d, 0, (0, 0), (0, 0)))


def swap_core(a):
    return send(a, moved(0, 1, (0, 0), (0, 0)))


def send_first(a, d):
    return send(a, moved(0, 0, (d, 0), (0, d)))


def send_second(a, d):
    return send(a, moved(0, 0, (0, d), (d, 0)))


def sync(*arrays):
    return lax.optimization_barrier(arrays)


def pick(a, index, axis):
    return lax.dynamic_index_in_dim(a, index % 4, axis=axis, keepdims=False)


def straight(a, move):
    return [move(a, 1), move(a, -1), move(a, 2)]


def total(arrays):
    return sum(v.astype(F32) for v in arrays).astype(BF)


def pass_on(plus, minus, flip):
    pairs = [p for k, d in ((0, 1), (1, -1)) for p in moved(d, 0, (0, 0), (0, 0)) if p[0] // 16 % 2 == k]
    return send(jnp.where(flip, minus, plus), pairs)


def regroup_kernel(cols_ref, order_ref, *refs):
    blocks, (near, far) = refs[:8], refs[8:]
    step = pl.program_id(0)

    @pl.when(step < 12)
    def _():
        for i in range(8):
            near[0, order_ref[i]] = blocks[i][0]

    @pl.when(step >= 12)
    def _():
        for i in range(8):
            far[0, order_ref[i]] = blocks[i][0]


def regroup(blocks, cols, order):
    count, rows, width = blocks[0].shape
    spec = pl.BlockSpec((1, rows, width), lambda j, c, o: (c[j], 0, 0))
    near_spec = pl.BlockSpec((1, 8, rows, width), lambda j, c, o: (jnp.minimum(j, 11), 0, 0, 0))
    far_spec = pl.BlockSpec((1, 8, rows, width), lambda j, c, o: (jnp.maximum(j - 12, 0), 0, 0, 0))
    return pl.pallas_call(
        regroup_kernel,
        grid_spec=pltpu.PrefetchScalarGridSpec(
            num_scalar_prefetch=2,
            grid=(count,),
            in_specs=[spec] * 8,
            out_specs=[near_spec, far_spec],
        ),
        out_shape=[
            jax.ShapeDtypeStruct((n, 8, rows, width), blocks[0].dtype) for n in (12, 4)
        ],
        compiler_params=pltpu.CompilerParams(vmem_limit_bytes=32 * 1024 * 1024),
        cost_estimate=pl.CostEstimate(
            flops=0, bytes_accessed=4 * 8 * count * rows * width, transcendentals=0
        ),
    )(cols, order, *blocks)


def body(iterate, route):
    rows, wide = iterate.shape
    groups, count, capacity = 8, 16, 42
    q = rows // groups
    width = wide // 2
    scale = 1.0 / (wide * groups)
    block = count * q
    ri, ci = lax.axis_index("row"), lax.axis_index("col")
    x, core, y, z = ri // 2, ri % 2, ci // 4, ci % 4
    flip = core == 1
    first, second = jnp.where(flip, z, y), jnp.where(flip, y, z)
    rows_rows = (((1,), (1,)), ((), ()))

    by_first = route.reshape(1, rows).astype(BF)
    by_first = jnp.stack([by_first, *straight(by_first, send_first)], axis=1)

    parts = iterate.reshape(groups, q, 2, width).transpose(0, 2, 1, 3)
    parts = lax.all_to_all(parts, "row", 0, 0, tiled=True).reshape(count, q, width)
    parts, by_first = sync(parts, by_first)
    targets = jnp.stack([by_first, *straight(by_first, send_second)], axis=0)
    targets = targets.reshape(count, rows)
    own = lax.all_to_all(parts, "col", 0, 0, tiled=True).reshape(block, width)
    own, route, targets = sync(own, route, targets)

    def gram(panel):
        part = lax.dot_general(panel, own, rows_rows, preferred_element_type=F32)
        return (part * scale).astype(BF).reshape(4, 4, q, block)

    def pick_first(parts, index, axis):
        return jnp.stack(
            [jnp.where(flip, pick(p, index, 1 - axis), pick(p, index, axis)) for p in parts], axis=0
        )

    def messages_first(parts):
        return [pick_first(parts, first + d, 0) for d in (1, -1, 2)]

    def deliver_first(messages):
        return [send_first(m, d) for m, d in zip(messages, (1, -1, 2))]

    def scatter_first(parts):
        return deliver_first(messages_first(parts))

    def gathered(parts, got):
        return total([pick_first(parts, first, 0), *got])

    steps = jnp.asarray([0, 1, 3, 2], jnp.int32)
    order = jnp.stack([((x - d) % 4) * 2 + (core ^ b) for d in (0, 1, 3, 2) for b in range(2)])
    first_of, second_of = (first - steps) % 4, (second - steps) % 4
    sources = jnp.where(
        flip,
        second_of[:, None] * 4 + first_of[None, :],
        first_of[None, :] * 4 + second_of[:, None],
    ).reshape(count)
    slots = capacity * count
    slot = lax.broadcasted_iota(jnp.int32, (slots, 1), 0)

    plus, minus = send_x(own, 1), send_x(own, -1)
    sibling = swap_core(own)
    grams = [gram(own), gram(sibling)]
    got = scatter_first(grams)

    shard = lax.broadcasted_iota(jnp.int32, (count, 1), 0)
    to_shard = (shard == sources[None, :]).astype(BF)
    targets = jnp.dot(to_shard, targets, preferred_element_type=F32).astype(jnp.int32)
    row_of = lax.broadcasted_iota(jnp.int32, (rows, 1), 0)
    upto = (row_of <= lax.broadcasted_iota(jnp.int32, (1, rows), 1)).astype(BF)

    def positions(match):
        counts = jnp.dot(match.astype(BF), upto, preferred_element_type=F32)
        return counts.astype(jnp.int32) - 1

    match = targets == ri
    by_panel = jnp.where(match, shard * capacity + positions(match), -1).reshape(count, groups, q)
    by_panel = jnp.take(by_panel, order, axis=1).swapaxes(0, 1).reshape(groups, block)
    labels = lax.broadcasted_iota(jnp.int32, (groups, 1), 0)
    match = route.reshape(1, rows) == labels
    row_slot = jnp.sum(jnp.where(match, labels * PAD + positions(match), 0), axis=0)
    row_slot = row_slot.reshape(1, rows)
    choose = (lax.broadcasted_iota(jnp.int32, (groups * PAD, 1), 0) == row_slot).astype(BF)

    def placed(i, panel):
        place = (slot == by_panel[i].reshape(1, block)).astype(BF)
        return jnp.dot(place, panel, preferred_element_type=F32)

    *got, plus, minus, by_panel, choose = sync(*got, plus, minus, by_panel, choose)
    sum_0 = gathered(grams, got)

    def put(sums, parts, d):
        for b in range(2):
            s = ((x - d) % 4) * 2 + (core ^ b)
            sums = lax.dynamic_update_index_in_dim(sums, parts[b], s, 0)
        return sums

    plus_s, minus_s = sync(swap_core(plus), swap_core(minus))
    far = pass_on(plus, minus, flip)
    grams = [gram(plus), gram(plus_s), gram(minus), gram(minus_s)]
    *messages, own_x, sibling_x = sync(*messages_first(grams), own, sibling)
    got = deliver_first(messages)
    mine = pick_first(grams, first, 0)
    update = placed(0, own_x)
    (update,) = sync(update)
    update = update + placed(1, sibling_x)
    sums = put(jnp.zeros((groups, 4, q, block), BF), sum_0, 0)
    *got_1, far, update, sums, mine = sync(*got, far, update, sums, mine)

    far_s = swap_core(far)
    grams = [gram(far), gram(far_s)]
    messages = messages_first(grams)
    *messages, plus_x, sibling_x, mine, g0, g1, g2 = sync(*messages, plus, plus_s, mine, *got_1)
    got = deliver_first(messages)
    sum_1 = total([mine, g0, g1, g2])
    sums = put(put(sums, sum_1[:2], 1), sum_1[2:], 3)
    update = update + placed(2, plus_x)
    (update,) = sync(update)
    update = update + placed(3, sibling_x)
    *got, update, sums = sync(*got, update, sums)
    sums = put(sums, gathered(grams, got), 2)

    messages = [pick(sums, second + d, 1) for d in (1, -1, 2)]
    *messages, minus_x, sibling_x = sync(*messages, minus, minus_s)
    got = [send_second(m, d) for m, d in zip(messages, (1, -1, 2))]
    update = update + placed(4, minus_x)
    (update,) = sync(update)
    update = update + placed(5, sibling_x)
    *got, update = sync(*got, update)
    share = total([pick(sums, second, 1), *got])
    gram_share = share.reshape(rows, block)

    routed = jnp.dot(choose, gram_share, preferred_element_type=F32).astype(BF)
    routed = routed.reshape(4, 2, PAD, block)
    other = swap_core(jnp.where(flip, routed[:, 0], routed[:, 1]))
    routed = jnp.stack([jnp.where(flip, routed[:, 1], routed[:, 0]), other], axis=1)
    *got, gram_share = sync(*[send_x(pick(routed, x + d, 0), d) for d in (1, -1, 2)], gram_share)
    lanes = [v[b] for v in (pick(routed, x, 0), *got) for b in range(2)]
    lanes = jnp.concatenate(lanes, axis=1)

    lanes, gram_share, far_x, sibling_x = sync(lanes, gram_share, far, far_s)
    got = straight(lanes, send_first)
    update = update + placed(6, far_x)
    (update,) = sync(update)
    update = update + placed(7, sibling_x)
    gram_p, gram_m = send_x(gram_share, 1), send_x(gram_share, -1)
    *got, gram_p, gram_m, gram_ps, gram_ms, update = sync(
        *got, gram_p, gram_m, swap_core(gram_p), swap_core(gram_m), update
    )

    top, low = jnp.concatenate([lanes, got[0]], axis=0), jnp.concatenate(got[1:], axis=0)
    top, low, gram_share = sync(top, low, gram_share)
    plus_t, minus_l = send_second(top, 1), send_second(low, -1)
    gram_f = send_x(gram_share, 2)
    gram_s, top_x, low_x = sync(swap_core(gram_share), top, low)
    plus_l, minus_t = send_second(low_x, 1), send_second(top_x, -1)
    far_t, far_l = send_second(plus_t, 1), send_second(minus_l, -1)
    gram_fs = swap_core(gram_f)
    gram_rows = jnp.concatenate(
        [gram_share, gram_s, gram_p, gram_ps, gram_m, gram_ms, gram_f, gram_fs], axis=1
    )
    place = (slot == by_panel.reshape(1, groups * block)).astype(BF)
    gram_cols = lax.dot_general(gram_rows, place, rows_rows, preferred_element_type=F32)
    gram_cols = gram_cols.astype(BF)

    def square_rows(chunk):
        term = lax.dot_general(chunk, gram_rows, rows_rows, preferred_element_type=F32)
        return term.astype(BF)

    terms = [square_rows(v) for v in (top, low, plus_t, plus_l, minus_t, minus_l)]
    far_t, far_l, gram_cols, gram_rows, *terms = sync(far_t, far_l, gram_cols, gram_rows, *terms)
    terms.append(square_rows(jnp.concatenate([far_t, far_l], axis=0)))

    source, position = slot // capacity, slot % capacity
    source_y, source_z = source // 4, source % 4
    away_first = (first - jnp.where(flip, source_z, source_y)) % 4
    away_second = (second - jnp.where(flip, source_y, source_z)) % 4
    away_first, away_second = away_first ^ (away_first >> 1), away_second ^ (away_second >> 1)
    column = (away_second * 4 + away_first) * PAD + position
    compact = (lax.broadcasted_iota(jnp.int32, (1, count * PAD), 1) == column).astype(BF)
    square = lax.dot_general(
        jnp.concatenate(terms, axis=0),
        compact,
        (((0,), (1,)), ((), ())),
        preferred_element_type=F32,
    )
    square = square.astype(BF).astype(F32)
    mixer = (coef_second * gram_cols.astype(F32) + coef_third * square).astype(BF)

    panels = [own, sibling, plus, plus_s, minus, minus_s, far, far_s]
    mixer, *panels = sync(mixer, *panels)
    near, away = regroup([v.reshape(count, q, width) for v in panels], sources, order)

    def product(chunk, panel):
        return lax.dot_general(
            chunk, panel, (((0,), (0,)), ((), ())), preferred_element_type=F32
        )

    *got, near, away = sync(*straight(mixer, send_first), near, away)
    near = near.reshape(6, 2 * rows, width)
    top, low = jnp.concatenate([mixer, got[0]], axis=0), jnp.concatenate(got[1:], axis=0)
    top, low = sync(top, low)
    plus_t, minus_l = send_second(top, 1), send_second(low, -1)
    plus_t, minus_l, own_t, own_l = sync(plus_t, minus_l, top, low)
    plus_l, minus_t = send_second(low, 1), send_second(top, -1)
    far_t, far_l = send_second(plus_t, 1), send_second(minus_l, -1)
    update = coef_first * update + product(own_t, near[0])
    for chunk, panel in ((own_l, near[1]), (plus_t, near[2]), (minus_l, near[5])):
        (update,) = sync(update)
        update = update + product(chunk, panel)
    plus_l, minus_t, update = sync(plus_l, minus_t, update)
    update = update + product(plus_l, near[3])
    (update,) = sync(update)
    update = update + product(minus_t, near[4])
    far_t, far_l, update = sync(far_t, far_l, update)
    update = update + product(jnp.concatenate([far_t, far_l], axis=0), away.reshape(4 * rows, width))
    return update.astype(BF)


def solution(mesh):
    in_specs = (P("col", "row"), P("col", None))
    out_specs = P("row", "col")
    return jax.shard_map(body, mesh=mesh, in_specs=in_specs, out_specs=out_specs, check_vma=False)
```

```python
import jax
import jax.numpy as jnp
from jax import lax
from jax.experimental import pallas as pl
from jax.experimental.pallas import tpu as pltpu
from jax.sharding import PartitionSpec as P

coef_first = 3.4445
coef_second = -4.775
coef_third = 2.0315

N_X, N_CORE, N_Y, N_Z = 4, 2, 4, 4
PAD = 48
BF = jnp.bfloat16
F32 = jnp.float32


def moved(dx, flip, dy, dz):
    pairs = []
    for x in range(4):
        for k in range(2):
            for y in range(4):
                for z in range(4):
                    to_row = ((x + dx) % 4) * 2 + (k ^ flip)
                    to_col = ((y + dy[k]) % 4) * 4 + (z + dz[k]) % 4
                    pairs.append(((x * 2 + k) * 16 + y * 4 + z, to_row * 16 + to_col))
    return pairs


def send(a, pairs):
    return lax.ppermute(a, ("row", "col"), pairs)


def send_x(a, d):
    return send(a, moved(d, 0, (0, 0), (0, 0)))


def swap_core(a):
    return send(a, moved(0, 1, (0, 0), (0, 0)))


def send_first(a, d):
    return send(a, moved(0, 0, (d, 0), (0, d)))


def send_second(a, d):
    return send(a, moved(0, 0, (0, d), (d, 0)))


def sync(*arrays):
    return lax.optimization_barrier(arrays)


def pick(a, index, axis):
    return lax.dynamic_index_in_dim(a, index % 4, axis=axis, keepdims=False)


def straight(a, move):
    return [move(a, 1), move(a, -1), move(a, 2)]


def total(arrays):
    return sum(v.astype(F32) for v in arrays).astype(BF)


def pass_on(plus, minus, flip):
    pairs = [p for k, d in ((0, 1), (1, -1)) for p in moved(d, 0, (0, 0), (0, 0)) if p[0] // 16 % 2 == k]
    return send(jnp.where(flip, minus, plus), pairs)


def regroup_kernel(cols_ref, order_ref, *refs):
    for i in range(8):
        refs[8][0, order_ref[i]] = refs[i][0]


def regroup(blocks, cols, order):
    _, rows, width = blocks[0].shape
    count = cols.shape[0]
    spec = pl.BlockSpec((1, rows, width), lambda j, c, o: (c[j], 0, 0))
    return pl.pallas_call(
        regroup_kernel,
        grid_spec=pltpu.PrefetchScalarGridSpec(
            num_scalar_prefetch=2,
            grid=(count,),
            in_specs=[spec] * 8,
            out_specs=pl.BlockSpec((1, 8, rows, width), lambda j, c, o: (j, 0, 0, 0)),
        ),
        out_shape=jax.ShapeDtypeStruct((count, 8, rows, width), blocks[0].dtype),
        compiler_params=pltpu.CompilerParams(vmem_limit_bytes=32 * 1024 * 1024),
        cost_estimate=pl.CostEstimate(
            flops=0, bytes_accessed=4 * 8 * count * rows * width, transcendentals=0
        ),
    )(cols, order, *blocks)


def body(iterate, route):
    rows, wide = iterate.shape
    groups, count, capacity = 8, 16, 42
    q = rows // groups
    width = wide // 2
    scale = 1.0 / (wide * groups)
    block = count * q
    ri, ci = lax.axis_index("row"), lax.axis_index("col")
    x, core, y, z = ri // 2, ri % 2, ci // 4, ci % 4
    flip = core == 1
    first, second = jnp.where(flip, z, y), jnp.where(flip, y, z)
    rows_rows = (((1,), (1,)), ((), ()))

    by_first = route.reshape(1, rows).astype(BF)
    by_first = jnp.stack([by_first, *straight(by_first, send_first)], axis=1)

    parts = iterate.reshape(groups, q, 2, width).transpose(0, 2, 1, 3)
    parts = lax.all_to_all(parts, "row", 0, 0, tiled=True).reshape(count, q, width)
    parts, by_first = sync(parts, by_first)
    targets = jnp.stack([by_first, *straight(by_first, send_second)], axis=0)
    targets = targets.reshape(count, rows)
    own = lax.all_to_all(parts, "col", 0, 0, tiled=True).reshape(block, width)
    own, route, targets = sync(own, route, targets)

    def gram(panel):
        part = lax.dot_general(panel, own, rows_rows, preferred_element_type=F32)
        return (part * scale).astype(BF).reshape(4, 4, q, block)

    def pick_first(parts, index, axis):
        return jnp.stack(
            [jnp.where(flip, pick(p, index, 1 - axis), pick(p, index, axis)) for p in parts], axis=0
        )

    def messages_first(parts):
        return [pick_first(parts, first + d, 0) for d in (1, -1, 2)]

    def deliver_first(messages):
        return [send_first(m, d) for m, d in zip(messages, (1, -1, 2))]

    def scatter_first(parts):
        return deliver_first(messages_first(parts))

    def gathered(parts, got):
        return total([pick_first(parts, first, 0), *got])

    steps = jnp.asarray([0, 1, 3, 2], jnp.int32)
    order = jnp.stack([((x - d) % 4) * 2 + (core ^ b) for d in (0, 1, 3, 2) for b in range(2)])
    first_of, second_of = (first - steps) % 4, (second - steps) % 4
    sources = jnp.where(
        flip,
        second_of[:, None] * 4 + first_of[None, :],
        first_of[None, :] * 4 + second_of[:, None],
    ).reshape(count)
    slots = capacity * count
    slot = lax.broadcasted_iota(jnp.int32, (slots, 1), 0)

    plus, minus = send_x(own, 1), send_x(own, -1)
    sibling = swap_core(own)
    grams = [gram(own), gram(sibling)]
    got = scatter_first(grams)

    shard = lax.broadcasted_iota(jnp.int32, (count, 1), 0)
    to_shard = (shard == sources[None, :]).astype(BF)
    targets = jnp.dot(to_shard, targets, preferred_element_type=F32).astype(jnp.int32)
    row_of = lax.broadcasted_iota(jnp.int32, (rows, 1), 0)
    upto = (row_of <= lax.broadcasted_iota(jnp.int32, (1, rows), 1)).astype(BF)

    def positions(match):
        counts = jnp.dot(match.astype(BF), upto, preferred_element_type=F32)
        return counts.astype(jnp.int32) - 1

    match = targets == ri
    by_panel = jnp.where(match, shard * capacity + positions(match), -1).reshape(count, groups, q)
    by_panel = jnp.take(by_panel, order, axis=1).swapaxes(0, 1).reshape(groups, block)
    labels = lax.broadcasted_iota(jnp.int32, (groups, 1), 0)
    match = route.reshape(1, rows) == labels
    row_slot = jnp.sum(jnp.where(match, labels * PAD + positions(match), 0), axis=0)
    row_slot = row_slot.reshape(1, rows)
    choose = (lax.broadcasted_iota(jnp.int32, (groups * PAD, 1), 0) == row_slot).astype(BF)

    def placed(i, panel):
        place = (slot == by_panel[i].reshape(1, block)).astype(BF)
        return jnp.dot(place, panel, preferred_element_type=F32)

    update = placed(0, own)
    (update,) = sync(update)
    update = update + placed(1, sibling)
    *got, plus, minus, by_panel, choose, update = sync(
        *got, plus, minus, by_panel, choose, update
    )
    sum_0 = gathered(grams, got)

    def put(sums, parts, d):
        for b in range(2):
            s = ((x - d) % 4) * 2 + (core ^ b)
            sums = lax.dynamic_update_index_in_dim(sums, parts[b], s, 0)
        return sums

    plus_s, minus_s = sync(swap_core(plus), swap_core(minus))
    far = pass_on(plus, minus, flip)
    grams = [gram(plus), gram(plus_s), gram(minus), gram(minus_s)]
    *messages, plus_x, sibling_x = sync(*messages_first(grams), plus, plus_s)
    got = deliver_first(messages)
    mine = pick_first(grams, first, 0)
    update = update + placed(2, plus_x)
    (update,) = sync(update)
    update = update + placed(3, sibling_x)
    sums = put(jnp.zeros((groups, 4, q, block), BF), sum_0, 0)
    *got_1, far, update, sums, mine = sync(*got, far, update, sums, mine)

    far_s = swap_core(far)
    grams = [gram(far), gram(far_s)]
    messages = messages_first(grams)
    *messages, mine, g0, g1, g2 = sync(*messages, mine, *got_1)
    got = deliver_first(messages)
    sum_1 = total([mine, g0, g1, g2])
    sums = put(put(sums, sum_1[:2], 1), sum_1[2:], 3)
    *got, sums = sync(*got, sums)
    sums = put(sums, gathered(grams, got), 2)

    messages = [pick(sums, second + d, 1) for d in (1, -1, 2)]
    *messages, minus_x, sibling_x = sync(*messages, minus, minus_s)
    got = [send_second(m, d) for m, d in zip(messages, (1, -1, 2))]
    update = update + placed(4, minus_x)
    (update,) = sync(update)
    update = update + placed(5, sibling_x)
    *got, update = sync(*got, update)
    share = total([pick(sums, second, 1), *got])
    gram_share = share.reshape(rows, block)

    routed = jnp.dot(choose, gram_share, preferred_element_type=F32).astype(BF)
    routed = routed.reshape(4, 2, PAD, block)
    other = swap_core(jnp.where(flip, routed[:, 0], routed[:, 1]))
    routed = jnp.stack([jnp.where(flip, routed[:, 1], routed[:, 0]), other], axis=1)
    *got, gram_share = sync(*[send_x(pick(routed, x + d, 0), d) for d in (1, -1, 2)], gram_share)
    lanes = [v[b] for v in (pick(routed, x, 0), *got) for b in range(2)]
    lanes = jnp.concatenate(lanes, axis=1)

    lanes, gram_share, far_x, sibling_x = sync(lanes, gram_share, far, far_s)
    got = straight(lanes, send_first)
    update = update + placed(6, far_x)
    (update,) = sync(update)
    update = update + placed(7, sibling_x)
    gram_p, gram_m = send_x(gram_share, 1), send_x(gram_share, -1)
    *got, gram_p, gram_m, gram_ps, gram_ms, update = sync(
        *got, gram_p, gram_m, swap_core(gram_p), swap_core(gram_m), update
    )

    top, low = jnp.concatenate([lanes, got[0]], axis=0), jnp.concatenate(got[1:], axis=0)
    top, low, gram_share = sync(top, low, gram_share)
    plus_t, minus_l = send_second(top, 1), send_second(low, -1)
    gram_f = send_x(gram_share, 2)
    gram_s, top_x, low_x = sync(swap_core(gram_share), top, low)
    plus_l, minus_t = send_second(low_x, 1), send_second(top_x, -1)
    far_t, far_l = send_second(plus_t, 1), send_second(minus_l, -1)
    gram_fs = swap_core(gram_f)
    gram_rows = jnp.concatenate(
        [gram_share, gram_s, gram_p, gram_ps, gram_m, gram_ms, gram_f, gram_fs], axis=1
    )
    place = (slot == by_panel.reshape(1, groups * block)).astype(BF)
    gram_cols = lax.dot_general(gram_rows, place, rows_rows, preferred_element_type=F32)
    gram_cols = gram_cols.astype(BF)

    def square_rows(chunk):
        term = lax.dot_general(chunk, gram_rows, rows_rows, preferred_element_type=F32)
        return term.astype(BF)

    terms = [square_rows(v) for v in (top, low, plus_t, plus_l, minus_t, minus_l)]
    panels = [own, sibling, plus, plus_s, minus, minus_s, far, far_s]
    panels = [v.reshape(count, q, width) for v in panels]
    _, _, *tied = sync(plus_l, minus_t, *panels)
    away = regroup(tied, sources[12:], order)
    far_t, far_l, gram_cols, gram_rows, away, *terms = sync(
        far_t, far_l, gram_cols, gram_rows, away, *terms
    )
    terms.append(square_rows(jnp.concatenate([far_t, far_l], axis=0)))

    source, position = slot // capacity, slot % capacity
    source_y, source_z = source // 4, source % 4
    away_first = (first - jnp.where(flip, source_z, source_y)) % 4
    away_second = (second - jnp.where(flip, source_y, source_z)) % 4
    away_first, away_second = away_first ^ (away_first >> 1), away_second ^ (away_second >> 1)
    column = (away_second * 4 + away_first) * PAD + position
    compact = (lax.broadcasted_iota(jnp.int32, (1, count * PAD), 1) == column).astype(BF)
    square = lax.dot_general(
        jnp.concatenate(terms, axis=0),
        compact,
        (((0,), (1,)), ((), ())),
        preferred_element_type=F32,
    )
    square = square.astype(BF).astype(F32)
    mixer = (coef_second * gram_cols.astype(F32) + coef_third * square).astype(BF)

    mixer, *tied = sync(mixer, *panels)
    near = regroup(tied, sources[:12], order)

    def product(chunk, panel):
        return lax.dot_general(
            chunk, panel, (((0,), (0,)), ((), ())), preferred_element_type=F32
        )

    *got, near = sync(*straight(mixer, send_first), near)
    near = near.reshape(6, 2 * rows, width)
    top, low = jnp.concatenate([mixer, got[0]], axis=0), jnp.concatenate(got[1:], axis=0)
    top, low = sync(top, low)
    plus_t, minus_l = send_second(top, 1), send_second(low, -1)
    plus_t, minus_l, own_t, own_l = sync(plus_t, minus_l, top, low)
    plus_l, minus_t = send_second(low, 1), send_second(top, -1)
    far_t, far_l = send_second(plus_t, 1), send_second(minus_l, -1)
    update = coef_first * update + product(own_t, near[0])
    for chunk, panel in ((own_l, near[1]), (plus_t, near[2]), (minus_l, near[5])):
        (update,) = sync(update)
        update = update + product(chunk, panel)
    plus_l, minus_t, update = sync(plus_l, minus_t, update)
    update = update + product(plus_l, near[3])
    (update,) = sync(update)
    update = update + product(minus_t, near[4])
    far_t, far_l, update = sync(far_t, far_l, update)
    update = update + product(jnp.concatenate([far_t, far_l], axis=0), away.reshape(4 * rows, width))
    return update.astype(BF)


def solution(mesh):
    in_specs = (P("col", "row"), P("col", None))
    out_specs = P("row", "col")
    return jax.shard_map(body, mesh=mesh, in_specs=in_specs, out_specs=out_specs, check_vma=False)
```

```python
import jax
import jax.numpy as jnp
from jax import lax
from jax.experimental import pallas as pl
from jax.experimental.pallas import tpu as pltpu
from jax.sharding import PartitionSpec as P

coef_first = 3.4445
coef_second = -4.775
coef_third = 2.0315

N_X, N_CORE, N_Y, N_Z = 4, 2, 4, 4
PAD = 48
BF = jnp.bfloat16
F32 = jnp.float32


def moved(dx, flip, dy, dz):
    pairs = []
    for x in range(4):
        for k in range(2):
            for y in range(4):
                for z in range(4):
                    to_row = ((x + dx) % 4) * 2 + (k ^ flip)
                    to_col = ((y + dy[k]) % 4) * 4 + (z + dz[k]) % 4
                    pairs.append(((x * 2 + k) * 16 + y * 4 + z, to_row * 16 + to_col))
    return pairs


def send(a, pairs):
    return lax.ppermute(a, ("row", "col"), pairs)


def send_x(a, d):
    return send(a, moved(d, 0, (0, 0), (0, 0)))


def swap_core(a):
    return send(a, moved(0, 1, (0, 0), (0, 0)))


def send_first(a, d):
    return send(a, moved(0, 0, (d, 0), (0, d)))


def send_second(a, d):
    return send(a, moved(0, 0, (0, d), (d, 0)))


def sync(*arrays):
    return lax.optimization_barrier(arrays)


def pick(a, index, axis):
    return lax.dynamic_index_in_dim(a, index % 4, axis=axis, keepdims=False)


def straight(a, move):
    return [move(a, 1), move(a, -1), move(a, 2)]


def total(arrays):
    return sum(v.astype(F32) for v in arrays).astype(BF)


def pass_on(plus, minus, flip):
    pairs = [p for k, d in ((0, 1), (1, -1)) for p in moved(d, 0, (0, 0), (0, 0)) if p[0] // 16 % 2 == k]
    return send(jnp.where(flip, minus, plus), pairs)


def regroup_kernel(cols_ref, order_ref, *refs):
    for i in range(8):
        refs[8][0, order_ref[i]] = refs[i][0]


def regroup(blocks, cols, order):
    _, rows, width = blocks[0].shape
    count = cols.shape[0]
    spec = pl.BlockSpec((1, rows, width), lambda j, c, o: (c[j], 0, 0))
    return pl.pallas_call(
        regroup_kernel,
        grid_spec=pltpu.PrefetchScalarGridSpec(
            num_scalar_prefetch=2,
            grid=(count,),
            in_specs=[spec] * 8,
            out_specs=pl.BlockSpec((1, 8, rows, width), lambda j, c, o: (j, 0, 0, 0)),
        ),
        out_shape=jax.ShapeDtypeStruct((count, 8, rows, width), blocks[0].dtype),
        compiler_params=pltpu.CompilerParams(vmem_limit_bytes=32 * 1024 * 1024),
        cost_estimate=pl.CostEstimate(
            flops=0, bytes_accessed=4 * 8 * count * rows * width, transcendentals=0
        ),
    )(cols, order, *blocks)


def body(iterate, route):
    rows, wide = iterate.shape
    groups, count, capacity = 8, 16, 42
    q = rows // groups
    width = wide // 2
    scale = 1.0 / (wide * groups)
    block = count * q
    ri, ci = lax.axis_index("row"), lax.axis_index("col")
    x, core, y, z = ri // 2, ri % 2, ci // 4, ci % 4
    flip = core == 1
    first, second = jnp.where(flip, z, y), jnp.where(flip, y, z)
    rows_rows = (((1,), (1,)), ((), ()))

    by_first = route.reshape(1, rows).astype(BF)
    by_first = jnp.stack([by_first, *straight(by_first, send_first)], axis=1)

    parts = iterate.reshape(groups, q, 2, width).transpose(0, 2, 1, 3)
    parts = lax.all_to_all(parts, "row", 0, 0, tiled=True).reshape(count, q, width)
    parts, by_first = sync(parts, by_first)
    targets = jnp.stack([by_first, *straight(by_first, send_second)], axis=0)
    targets = targets.reshape(count, rows)
    own = lax.all_to_all(parts, "col", 0, 0, tiled=True).reshape(block, width)
    own, route, targets = sync(own, route, targets)

    def gram(panel):
        part = lax.dot_general(panel, own, rows_rows, preferred_element_type=F32)
        return (part * scale).astype(BF).reshape(4, 4, q, block)

    def pick_first(parts, index, axis):
        return jnp.stack(
            [jnp.where(flip, pick(p, index, 1 - axis), pick(p, index, axis)) for p in parts], axis=0
        )

    def messages_first(parts):
        return [pick_first(parts, first + d, 0) for d in (1, -1, 2)]

    def deliver_first(messages):
        return [send_first(m, d) for m, d in zip(messages, (1, -1, 2))]

    def scatter_first(parts):
        return deliver_first(messages_first(parts))

    def gathered(parts, got):
        return total([pick_first(parts, first, 0), *got])

    steps = jnp.asarray([0, 1, 3, 2], jnp.int32)
    order = jnp.stack([((x - d) % 4) * 2 + (core ^ b) for d in (0, 1, 3, 2) for b in range(2)])
    first_of, second_of = (first - steps) % 4, (second - steps) % 4
    sources = jnp.where(
        flip,
        second_of[:, None] * 4 + first_of[None, :],
        first_of[None, :] * 4 + second_of[:, None],
    ).reshape(count)
    slots = capacity * count
    slot = lax.broadcasted_iota(jnp.int32, (slots, 1), 0)

    plus, minus = send_x(own, 1), send_x(own, -1)
    sibling = swap_core(own)
    grams = [gram(own), gram(sibling)]
    got = scatter_first(grams)

    shard = lax.broadcasted_iota(jnp.int32, (count, 1), 0)
    to_shard = (shard == sources[None, :]).astype(BF)
    targets = jnp.dot(to_shard, targets, preferred_element_type=F32).astype(jnp.int32)
    row_of = lax.broadcasted_iota(jnp.int32, (rows, 1), 0)
    upto = (row_of <= lax.broadcasted_iota(jnp.int32, (1, rows), 1)).astype(BF)

    def positions(match):
        counts = jnp.dot(match.astype(BF), upto, preferred_element_type=F32)
        return counts.astype(jnp.int32) - 1

    match = targets == ri
    by_panel = jnp.where(match, shard * capacity + positions(match), -1).reshape(count, groups, q)
    by_panel = jnp.take(by_panel, order, axis=1).swapaxes(0, 1).reshape(groups, block)
    labels = lax.broadcasted_iota(jnp.int32, (groups, 1), 0)
    match = route.reshape(1, rows) == labels
    row_slot = jnp.sum(jnp.where(match, labels * PAD + positions(match), 0), axis=0)
    row_slot = row_slot.reshape(1, rows)
    choose = (lax.broadcasted_iota(jnp.int32, (groups * PAD, 1), 0) == row_slot).astype(BF)

    def placed(i, panel):
        place = (slot == by_panel[i].reshape(1, block)).astype(BF)
        return jnp.dot(place, panel, preferred_element_type=F32)

    update = placed(0, own)
    (update,) = sync(update)
    update = update + placed(1, sibling)
    *got, plus, minus, by_panel, choose, update = sync(
        *got, plus, minus, by_panel, choose, update
    )
    sum_0 = gathered(grams, got)

    def put(sums, parts, d):
        for b in range(2):
            s = ((x - d) % 4) * 2 + (core ^ b)
            sums = lax.dynamic_update_index_in_dim(sums, parts[b], s, 0)
        return sums

    plus_s, minus_s = sync(swap_core(plus), swap_core(minus))
    far = pass_on(plus, minus, flip)
    grams = [gram(plus), gram(plus_s), gram(minus), gram(minus_s)]
    *messages, plus_x, sibling_x = sync(*messages_first(grams), plus, plus_s)
    got = deliver_first(messages)
    mine = pick_first(grams, first, 0)
    update = update + placed(2, plus_x)
    (update,) = sync(update)
    update = update + placed(3, sibling_x)
    sums = put(jnp.zeros((groups, 4, q, block), BF), sum_0, 0)
    *got_1, far, update, sums, mine = sync(*got, far, update, sums, mine)

    far_s = swap_core(far)
    grams = [gram(far), gram(far_s)]
    messages = messages_first(grams)
    *messages, mine, g0, g1, g2 = sync(*messages, mine, *got_1)
    got = deliver_first(messages)
    sum_1 = total([mine, g0, g1, g2])
    sums = put(put(sums, sum_1[:2], 1), sum_1[2:], 3)
    *got, sums = sync(*got, sums)
    sums = put(sums, gathered(grams, got), 2)

    messages = [pick(sums, second + d, 1) for d in (1, -1, 2)]
    *messages, minus_x, sibling_x = sync(*messages, minus, minus_s)
    got = [send_second(m, d) for m, d in zip(messages, (1, -1, 2))]
    update = update + placed(4, minus_x)
    (update,) = sync(update)
    update = update + placed(5, sibling_x)
    *got, update = sync(*got, update)
    share = total([pick(sums, second, 1), *got])
    gram_share = share.reshape(rows, block)

    routed = jnp.dot(choose, gram_share, preferred_element_type=F32).astype(BF)
    routed = routed.reshape(4, 2, PAD, block)
    other = swap_core(jnp.where(flip, routed[:, 0], routed[:, 1]))
    routed = jnp.stack([jnp.where(flip, routed[:, 1], routed[:, 0]), other], axis=1)
    *got, gram_share = sync(*[send_x(pick(routed, x + d, 0), d) for d in (1, -1, 2)], gram_share)
    lanes = [v[b] for v in (pick(routed, x, 0), *got) for b in range(2)]
    lanes = jnp.concatenate(lanes, axis=1)

    lanes, gram_share, far_x, sibling_x = sync(lanes, gram_share, far, far_s)
    got = straight(lanes, send_first)
    update = update + placed(6, far_x)
    (update,) = sync(update)
    update = update + placed(7, sibling_x)
    gram_p, gram_m = send_x(gram_share, 1), send_x(gram_share, -1)
    *got, gram_p, gram_m, gram_ps, gram_ms, update = sync(
        *got, gram_p, gram_m, swap_core(gram_p), swap_core(gram_m), update
    )

    top, low = jnp.concatenate([lanes, got[0]], axis=0), jnp.concatenate(got[1:], axis=0)
    top, low, gram_share = sync(top, low, gram_share)
    plus_t, minus_l = send_second(top, 1), send_second(low, -1)
    gram_f = send_x(gram_share, 2)
    gram_s, top_x, low_x = sync(swap_core(gram_share), top, low)
    plus_l, minus_t = send_second(low_x, 1), send_second(top_x, -1)
    far_t, far_l = send_second(plus_t, 1), send_second(minus_l, -1)
    gram_fs = swap_core(gram_f)
    gram_rows = jnp.concatenate(
        [gram_share, gram_s, gram_p, gram_ps, gram_m, gram_ms, gram_f, gram_fs], axis=1
    )
    place = (slot == by_panel.reshape(1, groups * block)).astype(BF)
    gram_cols = lax.dot_general(gram_rows, place, rows_rows, preferred_element_type=F32)
    gram_cols = gram_cols.astype(BF)

    def square_rows(chunk):
        term = lax.dot_general(chunk, gram_rows, rows_rows, preferred_element_type=F32)
        return term.astype(BF)

    terms = [square_rows(v) for v in (top, low, plus_t, plus_l, minus_t, minus_l)]
    panels = [own, sibling, plus, plus_s, minus, minus_s, far, far_s]
    panels = [v.reshape(count, q, width) for v in panels]
    _, _, *tied = sync(plus_l, minus_t, *panels)
    away = regroup(tied, sources[12:], order)
    far_t, far_l, gram_cols, gram_rows, away, *terms = sync(
        far_t, far_l, gram_cols, gram_rows, away, *terms
    )
    terms.append(square_rows(jnp.concatenate([far_t, far_l], axis=0)))

    source, position = slot // capacity, slot % capacity
    source_y, source_z = source // 4, source % 4
    away_first = (first - jnp.where(flip, source_z, source_y)) % 4
    away_second = (second - jnp.where(flip, source_y, source_z)) % 4
    away_first, away_second = away_first ^ (away_first >> 1), away_second ^ (away_second >> 1)
    column = (away_second * 4 + away_first) * PAD + position
    compact = (lax.broadcasted_iota(jnp.int32, (1, count * PAD), 1) == column).astype(BF)
    square = lax.dot_general(
        jnp.concatenate(terms, axis=0),
        compact,
        (((0,), (1,)), ((), ())),
        preferred_element_type=F32,
    )
    square = square.astype(BF).astype(F32)
    mixer = (coef_second * gram_cols.astype(F32) + coef_third * square).astype(BF)

    mixer, *tied = sync(mixer, *panels)
    near = regroup(tied, sources[:12], order)

    def product(chunk, panel):
        return lax.dot_general(
            chunk, panel, (((0,), (0,)), ((), ())), preferred_element_type=F32
        )

    *got, near = sync(*straight(mixer, send_first), near)
    near = near.reshape(6, 2 * rows, width)
    top, low = jnp.concatenate([mixer, got[0]], axis=0), jnp.concatenate(got[1:], axis=0)
    top, low = sync(top, low)
    plus_t, minus_l = send_second(top, 1), send_second(low, -1)
    update = coef_first * update + product(top, near[0])
    update, own_t, own_l = sync(update, top, low)
    plus_l, minus_t = send_second(own_l, 1), send_second(own_t, -1)
    far_t, far_l = send_second(plus_t, 1), send_second(minus_l, -1)
    for chunk, panel in ((own_l, near[1]), (plus_t, near[2]), (minus_l, near[5])):
        (update,) = sync(update)
        update = update + product(chunk, panel)
    plus_l, minus_t, update = sync(plus_l, minus_t, update)
    update = update + product(plus_l, near[3])
    (update,) = sync(update)
    update = update + product(minus_t, near[4])
    far_t, far_l, update = sync(far_t, far_l, update)
    update = update + product(jnp.concatenate([far_t, far_l], axis=0), away.reshape(4 * rows, width))
    return update.astype(BF)


def solution(mesh):
    in_specs = (P("col", "row"), P("col", None))
    out_specs = P("row", "col")
    return jax.shard_map(body, mesh=mesh, in_specs=in_specs, out_specs=out_specs, check_vma=False)
```

```python
import jax
import jax.numpy as jnp
from jax import lax
from jax.experimental import pallas as pl
from jax.experimental.pallas import tpu as pltpu
from jax.sharding import PartitionSpec as P

coef_first = 3.4445
coef_second = -4.775
coef_third = 2.0315

N_X, N_CORE, N_Y, N_Z = 4, 2, 4, 4
PAD = 48
BF = jnp.bfloat16
F32 = jnp.float32


def moved(dx, flip, dy, dz):
    pairs = []
    for x in range(4):
        for k in range(2):
            for y in range(4):
                for z in range(4):
                    to_row = ((x + dx) % 4) * 2 + (k ^ flip)
                    to_col = ((y + dy[k]) % 4) * 4 + (z + dz[k]) % 4
                    pairs.append(((x * 2 + k) * 16 + y * 4 + z, to_row * 16 + to_col))
    return pairs


def send(a, pairs):
    return lax.ppermute(a, ("row", "col"), pairs)


def send_x(a, d):
    return send(a, moved(d, 0, (0, 0), (0, 0)))


def swap_core(a):
    return send(a, moved(0, 1, (0, 0), (0, 0)))


def send_first(a, d):
    return send(a, moved(0, 0, (d, 0), (0, d)))


def send_second(a, d):
    return send(a, moved(0, 0, (0, d), (d, 0)))


def sync(*arrays):
    return lax.optimization_barrier(arrays)


def pick(a, index, axis):
    return lax.dynamic_index_in_dim(a, index % 4, axis=axis, keepdims=False)


def straight(a, move):
    return [move(a, 1), move(a, -1), move(a, 2)]


def total(arrays):
    return sum(v.astype(F32) for v in arrays).astype(BF)


def pass_on(plus, minus, flip):
    pairs = [p for k, d in ((0, 1), (1, -1)) for p in moved(d, 0, (0, 0), (0, 0)) if p[0] // 16 % 2 == k]
    return send(jnp.where(flip, minus, plus), pairs)


def regroup_kernel(cols_ref, order_ref, *refs):
    for i in range(8):
        refs[8][0, order_ref[i]] = refs[i][0]


def regroup(blocks, cols, order):
    _, rows, width = blocks[0].shape
    count = cols.shape[0]
    spec = pl.BlockSpec((1, rows, width), lambda j, c, o: (c[j], 0, 0))
    return pl.pallas_call(
        regroup_kernel,
        grid_spec=pltpu.PrefetchScalarGridSpec(
            num_scalar_prefetch=2,
            grid=(count,),
            in_specs=[spec] * 8,
            out_specs=pl.BlockSpec((1, 8, rows, width), lambda j, c, o: (j, 0, 0, 0)),
        ),
        out_shape=jax.ShapeDtypeStruct((count, 8, rows, width), blocks[0].dtype),
        compiler_params=pltpu.CompilerParams(vmem_limit_bytes=32 * 1024 * 1024),
        cost_estimate=pl.CostEstimate(
            flops=0, bytes_accessed=4 * 8 * count * rows * width, transcendentals=0
        ),
    )(cols, order, *blocks)


def body(iterate, route):
    rows, wide = iterate.shape
    groups, count, capacity = 8, 16, 42
    q = rows // groups
    width = wide // 2
    scale = 1.0 / (wide * groups)
    block = count * q
    ri, ci = lax.axis_index("row"), lax.axis_index("col")
    x, core, y, z = ri // 2, ri % 2, ci // 4, ci % 4
    flip = core == 1
    first, second = jnp.where(flip, z, y), jnp.where(flip, y, z)
    rows_rows = (((1,), (1,)), ((), ()))

    by_first = route.reshape(1, rows).astype(BF)
    by_first = jnp.stack([by_first, *straight(by_first, send_first)], axis=1)

    parts = iterate.reshape(groups, q, 2, width).transpose(0, 2, 1, 3)
    parts = lax.all_to_all(parts, "row", 0, 0, tiled=True).reshape(count, q, width)
    parts, by_first = sync(parts, by_first)
    targets = jnp.stack([by_first, *straight(by_first, send_second)], axis=0)
    targets = targets.reshape(count, rows)
    own = lax.all_to_all(parts, "col", 0, 0, tiled=True).reshape(block, width)
    own, route, targets = sync(own, route, targets)

    def gram(panel):
        part = lax.dot_general(panel, own, rows_rows, preferred_element_type=F32)
        return (part * scale).astype(BF).reshape(4, 4, q, block)

    def pick_first(parts, index, axis):
        return jnp.stack(
            [jnp.where(flip, pick(p, index, 1 - axis), pick(p, index, axis)) for p in parts], axis=0
        )

    def messages_first(parts):
        return [pick_first(parts, first + d, 0) for d in (1, -1, 2)]

    def deliver_first(messages):
        return [send_first(m, d) for m, d in zip(messages, (1, -1, 2))]

    def scatter_first(parts):
        return deliver_first(messages_first(parts))

    def gathered(parts, got):
        return total([pick_first(parts, first, 0), *got])

    steps = jnp.asarray([0, 1, 3, 2], jnp.int32)
    order = jnp.stack([((x - d) % 4) * 2 + (core ^ b) for d in (0, 1, 3, 2) for b in range(2)])
    first_of, second_of = (first - steps) % 4, (second - steps) % 4
    sources = jnp.where(
        flip,
        second_of[:, None] * 4 + first_of[None, :],
        first_of[None, :] * 4 + second_of[:, None],
    ).reshape(count)
    slots = capacity * count
    slot = lax.broadcasted_iota(jnp.int32, (slots, 1), 0)

    plus, minus = send_x(own, 1), send_x(own, -1)
    sibling = swap_core(own)
    grams = [gram(own), gram(sibling)]
    got = scatter_first(grams)

    shard = lax.broadcasted_iota(jnp.int32, (count, 1), 0)
    to_shard = (shard == sources[None, :]).astype(BF)
    targets = jnp.dot(to_shard, targets, preferred_element_type=F32).astype(jnp.int32)
    row_of = lax.broadcasted_iota(jnp.int32, (rows, 1), 0)
    upto = (row_of <= lax.broadcasted_iota(jnp.int32, (1, rows), 1)).astype(BF)

    def positions(match):
        counts = jnp.dot(match.astype(BF), upto, preferred_element_type=F32)
        return counts.astype(jnp.int32) - 1

    match = targets == ri
    by_panel = jnp.where(match, shard * capacity + positions(match), -1).reshape(count, groups, q)
    by_panel = jnp.take(by_panel, order, axis=1).swapaxes(0, 1).reshape(groups, block)
    labels = lax.broadcasted_iota(jnp.int32, (groups, 1), 0)
    match = route.reshape(1, rows) == labels
    row_slot = jnp.sum(jnp.where(match, labels * PAD + positions(match), 0), axis=0)
    row_slot = row_slot.reshape(1, rows)
    choose = (lax.broadcasted_iota(jnp.int32, (groups * PAD, 1), 0) == row_slot).astype(BF)

    def placed(i, panel):
        place = (slot == by_panel[i].reshape(1, block)).astype(BF)
        return jnp.dot(place, panel, preferred_element_type=F32)

    update = placed(0, own)
    (update,) = sync(update)
    update = update + placed(1, sibling)
    *got, plus, minus, by_panel, choose, update = sync(
        *got, plus, minus, by_panel, choose, update
    )
    sum_0 = gathered(grams, got)

    def put(sums, parts, d):
        for b in range(2):
            s = ((x - d) % 4) * 2 + (core ^ b)
            sums = lax.dynamic_update_index_in_dim(sums, parts[b], s, 0)
        return sums

    plus_s, minus_s = sync(swap_core(plus), swap_core(minus))
    far = pass_on(plus, minus, flip)
    grams = [gram(plus), gram(plus_s), gram(minus), gram(minus_s)]
    *messages, plus_x, sibling_x = sync(*messages_first(grams), plus, plus_s)
    got = deliver_first(messages)
    mine = pick_first(grams, first, 0)
    update = update + placed(2, plus_x)
    (update,) = sync(update)
    update = update + placed(3, sibling_x)
    sums = put(jnp.zeros((groups, 4, q, block), BF), sum_0, 0)
    *got_1, far, update, sums, mine = sync(*got, far, update, sums, mine)

    far_s = swap_core(far)
    grams = [gram(far), gram(far_s)]
    messages = messages_first(grams)
    *messages, mine, g0, g1, g2 = sync(*messages, mine, *got_1)
    got = deliver_first(messages)
    sum_1 = total([mine, g0, g1, g2])
    sums = put(put(sums, sum_1[:2], 1), sum_1[2:], 3)
    *got, sums = sync(*got, sums)
    sums = put(sums, gathered(grams, got), 2)

    messages = [pick(sums, second + d, 1) for d in (1, -1, 2)]
    *messages, minus_x, sibling_x = sync(*messages, minus, minus_s)
    got = [send_second(m, d) for m, d in zip(messages, (1, -1, 2))]
    update = update + placed(4, minus_x)
    (update,) = sync(update)
    update = update + placed(5, sibling_x)
    *got, update = sync(*got, update)
    share = total([pick(sums, second, 1), *got])
    gram_share = share.reshape(rows, block)

    routed = jnp.dot(choose, gram_share, preferred_element_type=F32).astype(BF)
    routed = routed.reshape(4, 2, PAD, block)
    other = swap_core(jnp.where(flip, routed[:, 0], routed[:, 1]))
    routed = jnp.stack([jnp.where(flip, routed[:, 1], routed[:, 0]), other], axis=1)
    *got, gram_share = sync(*[send_x(pick(routed, x + d, 0), d) for d in (1, -1, 2)], gram_share)
    lanes = [v[b] for v in (pick(routed, x, 0), *got) for b in range(2)]
    lanes = jnp.concatenate(lanes, axis=1)

    lanes, gram_share, far_x, sibling_x = sync(lanes, gram_share, far, far_s)
    got = straight(lanes, send_first)
    update = update + placed(6, far_x)
    (update,) = sync(update)
    update = update + placed(7, sibling_x)
    gram_p, gram_m = send_x(gram_share, 1), send_x(gram_share, -1)
    *got, gram_p, gram_m, gram_ps, gram_ms, update = sync(
        *got, gram_p, gram_m, swap_core(gram_p), swap_core(gram_m), update
    )

    top, low = jnp.concatenate([lanes, got[0]], axis=0), jnp.concatenate(got[1:], axis=0)
    top, low, gram_share = sync(top, low, gram_share)
    plus_t, minus_l = send_second(top, 1), send_second(low, -1)
    gram_f = send_x(gram_share, 2)
    gram_s, top_x, low_x = sync(swap_core(gram_share), top, low)
    plus_l, minus_t = send_second(low_x, 1), send_second(top_x, -1)
    far_t, far_l = send_second(plus_t, 1), send_second(minus_l, -1)
    gram_fs = swap_core(gram_f)
    gram_rows = jnp.concatenate(
        [gram_share, gram_s, gram_p, gram_ps, gram_m, gram_ms, gram_f, gram_fs], axis=1
    )
    place = (slot == by_panel.reshape(1, groups * block)).astype(BF)
    gram_cols = lax.dot_general(gram_rows, place, rows_rows, preferred_element_type=F32)
    gram_cols = gram_cols.astype(BF)

    def square_rows(chunk):
        term = lax.dot_general(chunk, gram_rows, rows_rows, preferred_element_type=F32)
        return term.astype(BF)

    terms = [square_rows(v) for v in (top, low, plus_t, plus_l, minus_t, minus_l)]
    panels = [own, sibling, plus, plus_s, minus, minus_s, far, far_s]
    panels = [v.reshape(count, q, width) for v in panels]
    _, _, *tied = sync(plus_l, minus_t, *panels)
    away = regroup(tied, sources[8:], order)
    far_t, far_l, gram_cols, gram_rows, away, *terms = sync(
        far_t, far_l, gram_cols, gram_rows, away, *terms
    )
    terms.append(square_rows(jnp.concatenate([far_t, far_l], axis=0)))

    source, position = slot // capacity, slot % capacity
    source_y, source_z = source // 4, source % 4
    away_first = (first - jnp.where(flip, source_z, source_y)) % 4
    away_second = (second - jnp.where(flip, source_y, source_z)) % 4
    away_first, away_second = away_first ^ (away_first >> 1), away_second ^ (away_second >> 1)
    column = (away_second * 4 + away_first) * PAD + position
    compact = (lax.broadcasted_iota(jnp.int32, (1, count * PAD), 1) == column).astype(BF)
    square = lax.dot_general(
        jnp.concatenate(terms, axis=0),
        compact,
        (((0,), (1,)), ((), ())),
        preferred_element_type=F32,
    )
    square = square.astype(BF).astype(F32)
    mixer = (coef_second * gram_cols.astype(F32) + coef_third * square).astype(BF)

    mixer, *tied = sync(mixer, *panels)
    near = regroup(tied, sources[:8], order)

    def product(chunk, panel):
        return lax.dot_general(
            chunk, panel, (((0,), (0,)), ((), ())), preferred_element_type=F32
        )

    *got, near = sync(*straight(mixer, send_first), near)
    near = near.reshape(4, 2 * rows, width)
    away = away.reshape(4, 2 * rows, width)
    top, low = jnp.concatenate([mixer, got[0]], axis=0), jnp.concatenate(got[1:], axis=0)
    top, low = sync(top, low)
    plus_t, minus_l = send_second(top, 1), send_second(low, -1)
    update = coef_first * update + product(top, near[0])
    update, own_t, own_l = sync(update, top, low)
    plus_l, minus_t = send_second(own_l, 1), send_second(own_t, -1)
    far_t, far_l = send_second(plus_t, 1), send_second(minus_l, -1)
    for chunk, panel in ((own_l, near[1]), (plus_t, near[2]), (minus_l, away[1])):
        (update,) = sync(update)
        update = update + product(chunk, panel)
    plus_l, minus_t, update = sync(plus_l, minus_t, update)
    update = update + product(plus_l, near[3])
    (update,) = sync(update)
    update = update + product(minus_t, away[0])
    far_t, far_l, update = sync(far_t, far_l, update)
    update = update + product(jnp.concatenate([far_t, far_l], axis=0), away[2:].reshape(4 * rows, width))
    return update.astype(BF)


def solution(mesh):
    in_specs = (P("col", "row"), P("col", None))
    out_specs = P("row", "col")
    return jax.shard_map(body, mesh=mesh, in_specs=in_specs, out_specs=out_specs, check_vma=False)
```

```python
import jax
import jax.numpy as jnp
from jax import lax
from jax.experimental import pallas as pl
from jax.experimental.pallas import tpu as pltpu
from jax.sharding import PartitionSpec as P

coef_first = 3.4445
coef_second = -4.775
coef_third = 2.0315

N_X, N_CORE, N_Y, N_Z = 4, 2, 4, 4
PAD = 48
BF = jnp.bfloat16
F32 = jnp.float32


def moved(dx, flip, dy, dz):
    pairs = []
    for x in range(4):
        for k in range(2):
            for y in range(4):
                for z in range(4):
                    to_row = ((x + dx) % 4) * 2 + (k ^ flip)
                    to_col = ((y + dy[k]) % 4) * 4 + (z + dz[k]) % 4
                    pairs.append(((x * 2 + k) * 16 + y * 4 + z, to_row * 16 + to_col))
    return pairs


def send(a, pairs):
    return lax.ppermute(a, ("row", "col"), pairs)


def send_x(a, d):
    return send(a, moved(d, 0, (0, 0), (0, 0)))


def swap_core(a):
    return send(a, moved(0, 1, (0, 0), (0, 0)))


def send_first(a, d):
    return send(a, moved(0, 0, (d, 0), (0, d)))


def send_second(a, d):
    return send(a, moved(0, 0, (0, d), (d, 0)))


def sync(*arrays):
    return lax.optimization_barrier(arrays)


def pick(a, index, axis):
    return lax.dynamic_index_in_dim(a, index % 4, axis=axis, keepdims=False)


def straight(a, move):
    return [move(a, 1), move(a, -1), move(a, 2)]


def total(arrays):
    return sum(v.astype(F32) for v in arrays).astype(BF)


def pass_on(plus, minus, flip):
    pairs = [p for k, d in ((0, 1), (1, -1)) for p in moved(d, 0, (0, 0), (0, 0)) if p[0] // 16 % 2 == k]
    return send(jnp.where(flip, minus, plus), pairs)


def regroup_kernel(cols_ref, order_ref, *refs):
    for i in range(8):
        refs[8][0, order_ref[i]] = refs[i][0]


def regroup(blocks, cols, order):
    _, rows, width = blocks[0].shape
    count = cols.shape[0]
    spec = pl.BlockSpec((1, rows, width), lambda j, c, o: (c[j], 0, 0))
    return pl.pallas_call(
        regroup_kernel,
        grid_spec=pltpu.PrefetchScalarGridSpec(
            num_scalar_prefetch=2,
            grid=(count,),
            in_specs=[spec] * 8,
            out_specs=pl.BlockSpec((1, 8, rows, width), lambda j, c, o: (j, 0, 0, 0)),
        ),
        out_shape=jax.ShapeDtypeStruct((count, 8, rows, width), blocks[0].dtype),
        compiler_params=pltpu.CompilerParams(vmem_limit_bytes=32 * 1024 * 1024),
        cost_estimate=pl.CostEstimate(
            flops=0, bytes_accessed=4 * 8 * count * rows * width, transcendentals=0
        ),
    )(cols, order, *blocks)


def body(iterate, route):
    rows, wide = iterate.shape
    groups, count, capacity = 8, 16, 42
    q = rows // groups
    width = wide // 2
    scale = 1.0 / (wide * groups)
    block = count * q
    ri, ci = lax.axis_index("row"), lax.axis_index("col")
    x, core, y, z = ri // 2, ri % 2, ci // 4, ci % 4
    flip = core == 1
    first, second = jnp.where(flip, z, y), jnp.where(flip, y, z)
    rows_rows = (((1,), (1,)), ((), ()))

    by_first = route.reshape(1, rows).astype(BF)
    by_first = jnp.stack([by_first, *straight(by_first, send_first)], axis=1)

    parts = iterate.reshape(groups, q, 2, width).transpose(0, 2, 1, 3)
    parts = lax.all_to_all(parts, "row", 0, 0, tiled=True).reshape(count, q, width)
    parts, by_first = sync(parts, by_first)
    targets = jnp.stack([by_first, *straight(by_first, send_second)], axis=0)
    targets = targets.reshape(count, rows)
    own = lax.all_to_all(parts, "col", 0, 0, tiled=True).reshape(block, width)
    own, route, targets = sync(own, route, targets)

    def gram(panel):
        part = lax.dot_general(panel, own, rows_rows, preferred_element_type=F32)
        return (part * scale).astype(BF).reshape(4, 4, q, block)

    def pick_first(parts, index, axis):
        return jnp.stack(
            [jnp.where(flip, pick(p, index, 1 - axis), pick(p, index, axis)) for p in parts], axis=0
        )

    def messages_first(parts):
        return [pick_first(parts, first + d, 0) for d in (1, -1, 2)]

    def deliver_first(messages):
        return [send_first(m, d) for m, d in zip(messages, (1, -1, 2))]

    def scatter_first(parts):
        return deliver_first(messages_first(parts))

    def gathered(parts, got):
        return total([pick_first(parts, first, 0), *got])

    steps = jnp.asarray([0, 1, 3, 2], jnp.int32)
    order = jnp.stack([((x - d) % 4) * 2 + (core ^ b) for d in (0, 1, 3, 2) for b in range(2)])
    first_of, second_of = (first - steps) % 4, (second - steps) % 4
    sources = jnp.where(
        flip,
        second_of[:, None] * 4 + first_of[None, :],
        first_of[None, :] * 4 + second_of[:, None],
    ).reshape(count)
    slots = capacity * count
    slot = lax.broadcasted_iota(jnp.int32, (slots, 1), 0)

    plus, minus = send_x(own, 1), send_x(own, -1)
    sibling = swap_core(own)
    grams = [gram(own), gram(sibling)]
    got = scatter_first(grams)

    shard = lax.broadcasted_iota(jnp.int32, (count, 1), 0)
    to_shard = (shard == sources[None, :]).astype(BF)
    targets = jnp.dot(to_shard, targets, preferred_element_type=F32).astype(jnp.int32)
    row_of = lax.broadcasted_iota(jnp.int32, (rows, 1), 0)
    upto = (row_of <= lax.broadcasted_iota(jnp.int32, (1, rows), 1)).astype(BF)

    def positions(match):
        counts = jnp.dot(match.astype(BF), upto, preferred_element_type=F32)
        return counts.astype(jnp.int32) - 1

    match = targets == ri
    by_panel = jnp.where(match, shard * capacity + positions(match), -1).reshape(count, groups, q)
    by_panel = jnp.take(by_panel, order, axis=1).swapaxes(0, 1).reshape(groups, block)
    labels = lax.broadcasted_iota(jnp.int32, (groups, 1), 0)
    match = route.reshape(1, rows) == labels
    row_slot = jnp.sum(jnp.where(match, labels * PAD + positions(match), 0), axis=0)
    row_slot = row_slot.reshape(1, rows)
    choose = (lax.broadcasted_iota(jnp.int32, (groups * PAD, 1), 0) == row_slot).astype(BF)

    def placed(i, panel):
        place = (slot == by_panel[i].reshape(1, block)).astype(BF)
        return jnp.dot(place, panel, preferred_element_type=F32)

    update = placed(0, own)
    (update,) = sync(update)
    update = update + placed(1, sibling)
    *got, plus, minus, by_panel, choose, update = sync(
        *got, plus, minus, by_panel, choose, update
    )
    sum_0 = gathered(grams, got)

    def put(sums, parts, d):
        for b in range(2):
            s = ((x - d) % 4) * 2 + (core ^ b)
            sums = lax.dynamic_update_index_in_dim(sums, parts[b], s, 0)
        return sums

    plus_s, minus_s = sync(swap_core(plus), swap_core(minus))
    far = pass_on(plus, minus, flip)
    grams = [gram(plus), gram(plus_s), gram(minus), gram(minus_s)]
    *messages, plus_x, sibling_x = sync(*messages_first(grams), plus, plus_s)
    got = deliver_first(messages)
    mine = pick_first(grams, first, 0)
    update = update + placed(2, plus_x)
    (update,) = sync(update)
    update = update + placed(3, sibling_x)
    sums = put(jnp.zeros((groups, 4, q, block), BF), sum_0, 0)
    *got_1, far, update, sums, mine = sync(*got, far, update, sums, mine)

    far_s = swap_core(far)
    grams = [gram(far), gram(far_s)]
    messages = messages_first(grams)
    *messages, mine, g0, g1, g2 = sync(*messages, mine, *got_1)
    got = deliver_first(messages)
    sum_1 = total([mine, g0, g1, g2])
    sums = put(put(sums, sum_1[:2], 1), sum_1[2:], 3)
    *got, sums = sync(*got, sums)
    sums = put(sums, gathered(grams, got), 2)

    messages = [pick(sums, second + d, 1) for d in (1, -1, 2)]
    *messages, minus_x, sibling_x = sync(*messages, minus, minus_s)
    got = [send_second(m, d) for m, d in zip(messages, (1, -1, 2))]
    update = update + placed(4, minus_x)
    (update,) = sync(update)
    update = update + placed(5, sibling_x)
    *got, update = sync(*got, update)
    share = total([pick(sums, second, 1), *got])
    gram_share = share.reshape(rows, block)

    routed = jnp.dot(choose, gram_share, preferred_element_type=F32).astype(BF)
    routed = routed.reshape(4, 2, PAD, block)
    other = swap_core(jnp.where(flip, routed[:, 0], routed[:, 1]))
    routed = jnp.stack([jnp.where(flip, routed[:, 1], routed[:, 0]), other], axis=1)
    *got, gram_share = sync(*[send_x(pick(routed, x + d, 0), d) for d in (1, -1, 2)], gram_share)
    lanes = [v[b] for v in (pick(routed, x, 0), *got) for b in range(2)]
    lanes = jnp.concatenate(lanes, axis=1)

    lanes, gram_share, far_x, sibling_x = sync(lanes, gram_share, far, far_s)
    got = straight(lanes, send_first)
    update = update + placed(6, far_x)
    (update,) = sync(update)
    update = update + placed(7, sibling_x)
    gram_p, gram_m = send_x(gram_share, 1), send_x(gram_share, -1)
    *got, gram_p, gram_m, gram_ps, gram_ms, update = sync(
        *got, gram_p, gram_m, swap_core(gram_p), swap_core(gram_m), update
    )

    top, low = jnp.concatenate([lanes, got[0]], axis=0), jnp.concatenate(got[1:], axis=0)
    top, low, gram_share = sync(top, low, gram_share)
    plus_t, minus_l = send_second(top, 1), send_second(low, -1)
    gram_f = send_x(gram_share, 2)
    gram_s, top_x, low_x = sync(swap_core(gram_share), top, low)
    plus_l, minus_t = send_second(low_x, 1), send_second(top_x, -1)
    far_t, far_l = send_second(plus_t, 1), send_second(minus_l, -1)
    gram_fs = swap_core(gram_f)
    gram_rows = jnp.concatenate(
        [gram_share, gram_s, gram_p, gram_ps, gram_m, gram_ms, gram_f, gram_fs], axis=1
    )
    place = (slot == by_panel.reshape(1, groups * block)).astype(BF)
    gram_cols = lax.dot_general(gram_rows, place, rows_rows, preferred_element_type=F32)
    gram_cols = gram_cols.astype(BF)

    def square_rows(chunk):
        term = lax.dot_general(chunk, gram_rows, rows_rows, preferred_element_type=F32)
        return term.astype(BF)

    terms = [square_rows(v) for v in (top, low, plus_t, plus_l, minus_t, minus_l)]
    panels = [own, sibling, plus, plus_s, minus, minus_s, far, far_s]
    panels = [v.reshape(count, q, width) for v in panels]
    _, _, *tied = sync(plus_l, minus_t, *panels)
    away = regroup(tied, sources[8:], order)
    far_t, far_l, gram_cols, gram_rows, away, *terms = sync(
        far_t, far_l, gram_cols, gram_rows, away, *terms
    )
    terms.append(square_rows(jnp.concatenate([far_t, far_l], axis=0)))

    source, position = slot // capacity, slot % capacity
    source_y, source_z = source // 4, source % 4
    away_first = (first - jnp.where(flip, source_z, source_y)) % 4
    away_second = (second - jnp.where(flip, source_y, source_z)) % 4
    away_first, away_second = away_first ^ (away_first >> 1), away_second ^ (away_second >> 1)
    column = (away_second * 4 + away_first) * PAD + position
    compact = (lax.broadcasted_iota(jnp.int32, (1, count * PAD), 1) == column).astype(BF)
    square = lax.dot_general(
        jnp.concatenate(terms, axis=0),
        compact,
        (((0,), (1,)), ((), ())),
        preferred_element_type=F32,
    )
    square = square.astype(BF).astype(F32)
    mixer = (coef_second * gram_cols.astype(F32) + coef_third * square).astype(BF)

    mixer, *tied = sync(mixer, *panels)
    near = regroup(tied, sources[:8], order)

    def product(chunk, panel):
        return lax.dot_general(
            chunk, panel, (((0,), (0,)), ((), ())), preferred_element_type=F32
        )

    *got, near = sync(*straight(mixer, send_first), near)
    near = near.reshape(4, 2 * rows, width)
    away = away.reshape(4, 2 * rows, width)
    top, low = jnp.concatenate([mixer, got[0]], axis=0), jnp.concatenate(got[1:], axis=0)
    top, low = sync(top, low)
    cut = slots // 2
    plus_l, minus_l = send_second(low, 1), send_second(low, -1)
    plus_t, minus_t = send_second(top, 1), send_second(top, -1)
    far_l = [send_second(plus_l[:, :cut], 1), send_second(minus_l[:, cut:], -1)]
    far_t = [send_second(plus_t[:, :cut], 1), send_second(minus_t[:, cut:], -1)]
    update = coef_first * update + product(low, near[1])
    for chunk, panel in ((top, near[0]), (plus_l, near[3]), (minus_l, away[1])):
        (update,) = sync(update)
        update = update + product(chunk, panel)
    plus_t, minus_t, update = sync(plus_t, minus_t, update)
    update = update + product(plus_t, near[2])
    (update,) = sync(update)
    update = update + product(minus_t, away[0])
    *far, update = sync(*far_l, *far_t, update)
    far = [jnp.concatenate(far[2:], axis=1), jnp.concatenate(far[:2], axis=1)]
    update = update + product(jnp.concatenate(far, axis=0), away[2:].reshape(4 * rows, width))
    return update.astype(BF)


def solution(mesh):
    in_specs = (P("col", "row"), P("col", None))
    out_specs = P("row", "col")
    return jax.shard_map(body, mesh=mesh, in_specs=in_specs, out_specs=out_specs, check_vma=False)
```
